256 devices in a mesh: dp: 16 (over x, y_hi, core), tile: 16 (over z, y_lo).
Axes of the slice: x: 4, y: 4 (y_hi: 2, y_lo: 2; y = y_hi * 2 + y_lo), z: 8, core: 2. Of those that a mesh axis runs over, the one named last changes fastest.
Arguments:
- frames: bfloat16 [16, 3, 16, 16, 2048], P('tile', None, None, None, 'dp'), may hold values from -9 to 9
- weights: bfloat16 [16, 64, 8, 972], P('tile'), may hold values from -0.1875 to 0.1875
- connect: int32 [16, 64, 8, 3], P('tile'), may hold values 0 or 1
Outputs:
- update: bfloat16 [16, 64, 8, 972], P('tile')
- loss_value: float32 [], replicated
The draws below stay inside these ranges and needn't reach their ends.
All inputs are finite; a program needn't handle non-finite values. No bound on the sum of `connect` on one device may be relied on, other than what follows from the above.
Results may differ from the reference program's by a relative error of at most 0.008.
Values may be sent and summed in bfloat16 or wider, within the bound.
A program may use at most 64 MiB of HBM per device.

```python
import jax
import jax.numpy as jnp
from jax import lax

FIELD = 18
MAPS = 8
STRIDE = 2
TILE_PX = 16
INPUTS = 972
HALO = 16
POS = 64
SIDE = 4
TILES = 16
BATCH = 2048


def draw_frames(key, part):
    subkeys = jax.random.split(jax.random.fold_in(key, 17), 3)
    shape = (TILES, 3, TILE_PX, TILE_PX, BATCH)
    tile_ids = jnp.arange(TILES).reshape(TILES, 1, 1, 1, 1)
    row_pos = jnp.arange(TILE_PX).reshape(1, 1, TILE_PX, 1, 1)
    col_pos = jnp.arange(TILE_PX).reshape(1, 1, 1, TILE_PX, 1)
    frame_pos = jnp.arange(BATCH).reshape(1, 1, 1, 1, BATCH)
    global_row = tile_ids // SIDE * TILE_PX + row_pos
    global_col = tile_ids % SIDE * TILE_PX + col_pos
    extent = SIDE * TILE_PX
    trend = 3.0 ** ((global_row + global_col).astype(jnp.float32) / (2.0 * extent) + frame_pos.astype(jnp.float32) / BATCH)
    rough = jax.random.uniform(subkeys[0], shape, jnp.float32, 0.6, 1.4)
    base = jnp.clip(jax.random.normal(subkeys[2], shape, jnp.float32), -2.0, 2.0)
    return (0.35 * trend * rough * base).astype(jnp.bfloat16)


def with_ends(entries, key, least, largest):
    shape = entries.shape
    spot = [jax.random.randint(jax.random.fold_in(key, axis), (), 0, shape[axis]) for axis in range(len(shape))]
    entries = entries.at[tuple(spot)].set(least)
    longest = shape.index(max(shape))
    spot[longest] = (spot[longest] + 1) % shape[longest]
    return entries.at[tuple(spot)].set(largest)


def block_scale(own_key, dims, shards, smallest, top_value):
    factor_of = 1.0
    for dim, blocks in shards:
        heights = jax.random.uniform(jax.random.fold_in(jax.random.fold_in(own_key, 6), dim), (blocks,), jnp.float32, smallest / len(shards), top_value / len(shards))
        factor_of = factor_of * jnp.repeat(jnp.exp(heights), dims[dim] // blocks).reshape((-1,) + (1,) * (len(dims) - 1 - dim))
    return factor_of


def normal_values(own_key, shape, deviation, reach, shards=(), kind=jnp.bfloat16):
    values = deviation * jax.random.normal(own_key, shape, jnp.float32)
    if shards:
        values = values * block_scale(own_key, shape, shards, -0.22, 0.18)
    return jnp.clip(values, -reach, reach).astype(kind)


def setup_inputs(seed: int = 0) -> dict:
    streams_of = jax.random.split(jax.random.key(seed), 4)
    return {
        "frames": draw_frames(jax.random.fold_in(streams_of[3], 71), 0),
        "weights": normal_values(streams_of[1], (TILES, POS, MAPS, INPUTS), INPUTS ** -0.5, 0.1875, ((0, 16),)),
        "connect": with_ends((jax.random.randint(streams_of[2], (TILES, POS, MAPS, 3), 0, 4) < 3).astype(jnp.int32), jax.random.fold_in(streams_of[2], 1), 0, 1),
    }


sparsity_weight = 1.0
smooth_eps = 0.01
guard_eps = 1e-06

def masked(values, connect):
    blocked = values.reshape(values.shape[0], POS, MAPS, 3, FIELD * FIELD)
    opened = connect.astype(values.dtype)[..., None]
    return (blocked * opened).reshape(values.shape)

def patch_block(extended, row_index):
    strip_rows = lax.dynamic_slice_in_dim(extended, (row_index * STRIDE).astype(jnp.int32), FIELD, 1)
    pieces = [strip_rows[:, :, column * STRIDE:column * STRIDE + FIELD] for column in range(TILE_PX // STRIDE)]
    blocks = jnp.stack(pieces, 0)
    return blocks.reshape(blocks.shape[0], INPUTS, blocks.shape[-1])

def spread(coeffs, span_px):
    shaped = coeffs.reshape(coeffs.shape[0], 3, FIELD, FIELD, coeffs.shape[-1])
    canvas_strip = jnp.zeros((3, FIELD, span_px, coeffs.shape[-1]), jnp.float32)
    for column in range(TILE_PX // STRIDE):
        canvas_strip = canvas_strip.at[:, :, column * STRIDE:column * STRIDE + FIELD].add(shaped[column])
    return canvas_strip

def neighbour_ids(tile_index):
    right_id = ((tile_index + 1) % TILES).astype(jnp.int32)
    below_id = ((tile_index + SIDE) % TILES).astype(jnp.int32)
    corner_id = ((tile_index + SIDE + 1) % TILES).astype(jnp.int32)
    return (right_id, below_id, corner_id)

def pick_tile(stack, index):
    return lax.dynamic_index_in_dim(stack, index.astype(jnp.int32), 0, keepdims=False)

def extended_tile(stack, tile_index):
    right_id, below_id, corner_id = neighbour_ids(tile_index)
    upper = jnp.concatenate([pick_tile(stack, tile_index), pick_tile(stack, right_id)[:, :, :HALO]], axis=2)
    lower = jnp.concatenate([pick_tile(stack, below_id)[:, :HALO], pick_tile(stack, corner_id)[:, :HALO, :HALO]], axis=2)
    return jnp.concatenate([upper, lower], axis=1)

def add_region(canvas, index, row_lo, col_lo, piece):
    current = pick_tile(canvas, index)
    current = current.at[:, row_lo:row_lo + piece.shape[1], col_lo:col_lo + piece.shape[2]].add(piece)
    return lax.dynamic_update_index_in_dim(canvas, current, index.astype(jnp.int32), 0)

def reference(frames, weights, connect):
    frames_total = frames.shape[-1]
    rows_out = TILE_PX // STRIDE
    span_px = TILE_PX + HALO
    effective = masked(weights, connect).reshape(TILES, rows_out, rows_out, MAPS, INPUTS)

    def encode_tile(canvas, tile_index):
        extended = extended_tile(frames, tile_index)
        weight_rows = effective[tile_index]

        def row_step(canvas_part, row_index):
            blocks = patch_block(extended, row_index)
            w_row = weight_rows[row_index].astype(jnp.float32)
            coded = jnp.einsum('cmk,ckb->cmb', w_row, blocks.astype(jnp.float32))
            rounded = coded.astype(jnp.bfloat16).astype(jnp.float32)
            decoded = jnp.einsum('cmk,cmb->ckb', w_row, rounded)
            start = (row_index * STRIDE).astype(jnp.int32)
            window = lax.dynamic_slice_in_dim(canvas_part, start, FIELD, 1)
            canvas_part = lax.dynamic_update_slice_in_dim(canvas_part, window + spread(decoded, span_px), start, 1)
            return (canvas_part, coded)
        canvas_part, coded = lax.scan(row_step, jnp.zeros((3, span_px, span_px, frames_total), jnp.float32), jnp.arange(rows_out, dtype=jnp.int32))
        right_id, below_id, corner_id = neighbour_ids(tile_index)
        canvas = add_region(canvas, tile_index, 0, 0, canvas_part[:, :TILE_PX, :TILE_PX])
        canvas = add_region(canvas, right_id, 0, 0, canvas_part[:, :TILE_PX, TILE_PX:])
        canvas = add_region(canvas, below_id, 0, 0, canvas_part[:, TILE_PX:, :TILE_PX])
        canvas = add_region(canvas, corner_id, 0, 0, canvas_part[:, TILE_PX:, TILE_PX:])
        return (canvas, coded)
    canvas, coded_all = lax.scan(encode_tile, jnp.zeros((TILES, 3, TILE_PX, TILE_PX, frames_total), jnp.float32), jnp.arange(TILES, dtype=jnp.int32))
    errors = canvas - frames.astype(jnp.float32)
    error_sq = jnp.sum(errors * errors)
    sparse = jnp.sum(jnp.sqrt(smooth_eps + coded_all * coded_all))
    error_tiles = errors.astype(jnp.bfloat16)

    def grad_tile(unused, inputs):
        tile_index, coded_tile = inputs
        ext_frames = extended_tile(frames, tile_index)
        ext_errors = extended_tile(error_tiles, tile_index)
        weight_rows = effective[tile_index]

        def row_step(inner, pair):
            row_index, coded = pair
            frame_block = patch_block(ext_frames, row_index).astype(jnp.float32)
            error_block = patch_block(ext_errors, row_index).astype(jnp.float32)
            w_row = weight_rows[row_index].astype(jnp.float32)
            encoded_err = jnp.einsum('cmk,ckb->cmb', w_row, error_block)
            left_coef = (2.0 * coded).astype(jnp.bfloat16).astype(jnp.float32)
            right_coef = (2.0 * encoded_err + sparsity_weight * coded / jnp.sqrt(smooth_eps + coded * coded)).astype(jnp.bfloat16).astype(jnp.float32)
            grad_row = jnp.einsum('cmb,ckb->cmk', left_coef, error_block) + jnp.einsum('cmb,ckb->cmk', right_coef, frame_block)
            return (inner, grad_row)
        inner, grad_rows = lax.scan(row_step, unused, (jnp.arange(rows_out, dtype=jnp.int32), coded_tile))
        return (inner, grad_rows.reshape(POS, MAPS, INPUTS))
    unused, gradients = lax.scan(grad_tile, jnp.zeros((), jnp.float32), (jnp.arange(TILES, dtype=jnp.int32), coded_all))
    gradients = masked(gradients, connect)
    mean_sq = jnp.sum(gradients * gradients) / (TILES * POS * MAPS * INPUTS)
    update = (-(gradients * lax.rsqrt(mean_sq + guard_eps))).astype(jnp.bfloat16)
    loss_value = ((error_sq + sparsity_weight * sparse) / frames_total).astype(jnp.float32)
    return (update, loss_value)
```

```python
import functools

import jax
import jax.numpy as jnp
from jax import lax
from jax.experimental import pallas as pl
from jax.experimental.pallas import tpu as pltpu
from jax.sharding import PartitionSpec as P

FIELD = 18
MAPS = 8
INPUTS = 972
POS = 64
PX = 16
BLOCK = 640
BAND = 3 * BLOCK
ROWS = POS * MAPS
WIDE = 1024
GROUPS = 4
MESH = pl.DeviceIdType.MESH
F32 = jnp.float32
BF16 = jnp.bfloat16

smooth_eps = 0.01
guard_eps = 1e-06


def dot(a, b):
    return lax.dot_general(a, b, (((1,), (0,)), ((), ())), preferred_element_type=F32)


def dot_nt(a, b):
    return lax.dot_general(a, b, (((1,), (1,)), ((), ())), preferred_element_type=F32)


def kernel(
    n_dp, n_tile, batch, side,
    frames_ref, w_ref, conn_ref,
    out_ref, loss_ref,
    place, wpad, band, band_t, xext, eext, coded, coded_b, enc, dec,
    right_src, right_in, corner_src, corner_in, below_src, below_in,
    grad, gband, gsend, rs_in, rs_half, rs_parts, gathered,
    squares, scal_a, scal_a_in, scal_b, scal_b_in,
    x_send, x_recv, f_send, f_recv, e_send, e_recv,
    rs1_send, rs1_recv, rs2_send, rs2_recv, a_send, a_recv, ag_send, ag_recv, fw_send, fw_recv,
    b_send, b_recv,
):
    d = lax.axis_index("dp")
    t = lax.axis_index("tile")
    n_chip = n_dp // 2
    core = lax.rem(d, 2)
    chip = lax.div(d, 2)
    left = (d, lax.rem(t + n_tile - 1, n_tile))
    right = (d, lax.rem(t + 1, n_tile))
    above = (d, lax.rem(t + n_tile - side, n_tile))
    below = (d, lax.rem(t + side, n_tile))
    sibling = (d + 1 - 2 * core, t)

    barrier = pltpu.get_barrier_semaphore()

    @pl.loop(1, n_dp)
    def _(o):
        pl.semaphore_signal(barrier, inc=1, device_id=(lax.rem(d + o, n_dp), t), device_id_type=MESH)

    @pl.loop(1, n_tile)
    def _(o):
        pl.semaphore_signal(barrier, inc=1, device_id=(d, lax.rem(t + o, n_tile)), device_id_type=MESH)

    pl.semaphore_wait(barrier, n_dp + n_tile - 2)

    def remote(src, dst, send, recv, device):
        return pltpu.make_async_remote_copy(
            src_ref=src, dst_ref=dst, send_sem=send, recv_sem=recv, device_id=device, device_id_type=MESH
        )

    def halo(own, ext, send, recv):
        def quarter(c, low, far):
            return ext.at[pl.ds(c * 32 + PX * low, PX), pl.ds(PX * far, PX)]

        to_left = [remote(own(c), quarter(c, 0, 1), send.at[c], recv.at[c], left) for c in range(3)]
        to_above = [remote(own(c), quarter(c, 1, 0), send.at[3 + c], recv.at[3 + c], above) for c in range(3)]
        relay = [
            remote(quarter(c, 1, 0), quarter(c, 1, 1), send.at[6 + c], recv.at[6 + c], left)
            for c in range(3)
        ]
        return to_left, to_above, relay

    x_left, x_above, x_relay = halo(lambda c: frames_ref.at[c], xext, x_send, x_recv)
    for c in range(3):
        x_above[c].start()
        x_left[c].start()
    for c in range(3):
        xext[pl.ds(c * 32, PX), pl.ds(0, PX)] = frames_ref[c]

    lane = lax.broadcasted_iota(jnp.int32, (1, BAND), 1)
    chan = jnp.where(lane >= BLOCK, 1, 0) + jnp.where(lane >= 2 * BLOCK, 1, 0)
    spot = lane - BLOCK * chan
    prow = spot >> 5
    pcol = spot & 31
    source = jnp.where((pcol < FIELD) & (prow < FIELD), FIELD * FIELD * chan + FIELD * prow + pcol, -1)

    @pl.loop(0, WIDE // 32)
    def _(b):
        number = lax.broadcasted_iota(jnp.int32, (32, BAND), 0) + b * 32
        place[pl.ds(b * 32, 32), :] = jnp.where(number == source, 1.0, 0.0).astype(BF16)

    wpad[:, pl.ds(896, 128)] = jnp.zeros((128, 128), BF16)

    def open_map(g, c):
        return conn_ref[pl.ds(g * 16, 16), :, c : c + 1].astype(F32).reshape(128, 1)

    @pl.loop(0, GROUPS)
    def _(g):
        wpad[:, pl.ds(0, INPUTS)] = w_ref[pl.ds(g * 16, 16)].astype(F32).reshape(128, INPUTS).astype(BF16)
        for c in range(3):
            lanes = pl.ds(c * BLOCK, BLOCK)
            lo, hi = ((0, 384), (256, 768), (640, 1024))[c]
            spread = dot(wpad[:, lo:hi], place[lo:hi, lanes]) * open_map(g, c)
            rolled = []
            for p in range(16):
                shift = 64 * (p // 8) + 2 * (p % 8)
                part = spread[p * 8 : p * 8 + 8]
                rolled.append(pltpu.roll(part, shift, 1) if shift else part)
            whole = jnp.concatenate(rolled, axis=0)
            band[pl.ds(g * 128, 128), lanes] = whole.astype(BF16)
            band_t[g, lanes, :] = whole.T.astype(BF16)

    def strip(ext, g, c):
        return ext[pl.ds(c * 32 + 4 * g, 20)].reshape(BLOCK, 128)

    for c in range(3):
        x_above[c].wait_recv()
        x_relay[c].start()
    for c in range(3):
        x_left[c].wait_recv()
        x_relay[c].wait_recv()

        @pl.loop(0, GROUPS)
        def _(g):
            rows = pl.ds(g * 128, 128)
            term = dot(band[rows, c * BLOCK : (c + 1) * BLOCK], strip(xext, g, c))
            if c == 0:
                coded[rows] = term
            else:
                total = coded[rows] + term
                coded[rows] = total
                if c == 2:
                    coded_b[rows] = total.astype(BF16)

    fold_corner = [remote(corner_src.at[c], corner_in.at[c], f_send.at[c], f_recv.at[c], right) for c in range(3)]
    fold_right = [remote(right_src.at[c], right_in.at[c], f_send.at[3 + c], f_recv.at[3 + c], right) for c in range(3)]
    fold_below = [remote(below_src.at[c], below_in.at[c], f_send.at[6 + c], f_recv.at[6 + c], below) for c in range(3)]

    dec[...] = jnp.zeros(dec.shape, F32)
    for c in range(3):

        @pl.loop(0, GROUPS)
        def _(g):
            term = dot(band_t[g, c * BLOCK : (c + 1) * BLOCK, :], coded_b[pl.ds(g * 128, 128)])
            dec[pl.ds(c * 32 + 4 * g, 20)] += term.reshape(20, 32, 128)

        corner_src[c] = dec[pl.ds(c * 32 + PX, PX), pl.ds(PX, PX)].astype(BF16)
        fold_corner[c].start()
        right_src[c] = dec[pl.ds(c * 32, PX), pl.ds(PX, PX)].astype(BF16)
    for c in range(3):
        fold_corner[c].wait_recv()
        summed = dec[pl.ds(c * 32 + PX, PX), pl.ds(0, PX)] + corner_in[c].astype(F32)
        below_src[c] = summed.astype(BF16)
        fold_below[c].start()
        fold_right[c].start()

    value = coded[...]
    penalty = jnp.sqrt(smooth_eps + value * value)
    squares[3:] = jnp.zeros((5, 8, 128), F32)
    squares[2] = jnp.sum(penalty.reshape(ROWS // 8, 8, 128), axis=0)

    e_left, e_above, e_relay = halo(lambda c: eext.at[pl.ds(c * 32, PX), pl.ds(0, PX)], eext, e_send, e_recv)
    error_sq = jnp.zeros((16, 128), F32)
    for c in range(3):
        fold_right[c].wait_recv()
        fold_below[c].wait_recv()
        own = pl.ds(c * 32, PX)
        rebuilt = dec[own, pl.ds(0, PX)] + right_in[c].astype(F32) + below_in[c].astype(F32)
        error = rebuilt - frames_ref[c].astype(F32)
        error_sq = error_sq + jnp.sum(error * error, axis=0)
        eext[own, pl.ds(0, PX)] = error.astype(BF16)
        e_above[c].start()
        e_left[c].start()
    squares[1] = error_sq[:8] + error_sq[8:]

    for c in range(3):
        e_above[c].wait_recv()
        e_relay[c].start()
    for c in range(3):
        e_left[c].wait_recv()
        e_relay[c].wait_recv()

        @pl.loop(0, GROUPS)
        def _(g):
            rows = pl.ds(g * 128, 128)
            lanes = slice(c * BLOCK, (c + 1) * BLOCK)
            errors = strip(eext, g, c)
            term = dot(band[rows, lanes], errors)
            if c == 0:
                enc[rows] = term
            else:
                enc[rows] += term
            grad[rows, lanes] = dot_nt(coded_b[rows] * 2, errors)

    def finish(g):
        rows = pl.ds(pl.multiple_of(g * 128, 128), 128)
        value = coded[rows]
        coef = (2.0 * enc[rows] + value * lax.rsqrt(smooth_eps + value * value)).astype(BF16)
        for c in range(3):
            lanes = slice(c * BLOCK, (c + 1) * BLOCK)
            whole = (grad[rows, lanes] + dot_nt(coef, strip(xext, g, c))) * open_map(g, c)
            rolled = []
            for p in range(16):
                shift = 64 * (p // 8) + 2 * (p % 8)
                part = whole[p * 8 : p * 8 + 8]
                rolled.append(pltpu.roll(part, BLOCK - shift, 1) if shift else part)
            gband[:, lanes] = jnp.concatenate(rolled, axis=0).astype(BF16)
        gsend[rows] = dot_nt(gband[...], place[...]).astype(BF16)

    half = ROWS // 2
    piece = half // n_chip
    swap = []
    for s in range(2):
        g = 2 * (1 - core) + s
        finish(g)
        copy = remote(
            gsend.at[pl.ds(pl.multiple_of(g * 128, 128), 128)], rs_in.at[s], rs1_send.at[s], rs1_recv.at[s], sibling
        )
        copy.start()
        swap.append(copy)
    for s in range(2):
        g = 2 * core + s
        finish(g)
    for s in range(2):
        g = 2 * core + s
        swap[s].wait_recv()
        both = gsend[pl.ds(pl.multiple_of(g * 128, 128), 128)].astype(F32) + rs_in[s].astype(F32)
        rs_half[pl.ds(s * 4, 4)] = both.astype(BF16).reshape(4, piece, WIDE)

    scatter = []
    for o in range(1, n_chip):
        to = lax.rem(chip + o, n_chip)
        copy = remote(rs_half.at[to], rs_parts.at[o - 1], rs2_send.at[o - 1], rs2_recv.at[o - 1], (2 * to + core, t))
        copy.start()
        scatter.append(copy)
    share = rs_half[chip].astype(F32)
    for o in range(1, n_chip):
        scatter[o - 1].wait_recv()
        share = share + rs_parts[o - 1].astype(F32)

    def rows_of(k):
        return pl.ds(pl.multiple_of(core * half + k * piece, piece), piece)

    gathered[rows_of(chip)] = share.astype(BF16)
    square = share * share
    folded = square[:, :128]
    for b in range(1, WIDE // 128):
        folded = folded + square[:, b * 128 : (b + 1) * 128]
    squares[0] = jnp.sum(folded.reshape(piece // 8, 8, 128), axis=0)

    scal_a[...] = jnp.sum(squares[...], axis=1)
    to_dp = []
    for o in range(1, n_dp):
        to = lax.rem(d + o, n_dp)
        copy = remote(scal_a, scal_a_in.at[o - 1], a_send.at[o - 1], a_recv.at[o - 1], (to, t))
        copy.start()
        to_dp.append(copy)
    spread_out = []
    own_share = gathered.at[rows_of(chip)]
    for o in range(1, n_chip):
        to = lax.rem(chip + o, n_chip)
        copy = remote(own_share, own_share, ag_send.at[o - 1], ag_recv.at[o - 1], (2 * to + core, t))
        copy.start()
        spread_out.append(copy)
    forward = [remote(own_share, own_share, fw_send.at[0], fw_recv.at[0], sibling)]
    forward[0].start()

    total = scal_a[...]
    for o in range(1, n_dp):
        to_dp[o - 1].wait_recv()
        total = total + scal_a_in[o - 1]
    scal_b[...] = total
    to_tiles = []
    for o in range(1, n_tile):
        to = lax.rem(t + o, n_tile)
        copy = remote(scal_b, scal_b_in.at[o - 1], b_send.at[o - 1], b_recv.at[o - 1], (d, to))
        copy.start()
        to_tiles.append(copy)
    for o in range(1, n_chip):
        origin = lax.rem(chip + n_chip - o, n_chip)
        arrived = gathered.at[rows_of(origin)]
        spread_out[o - 1].wait_recv()
        copy = remote(arrived, arrived, fw_send.at[o], fw_recv.at[o], sibling)
        copy.start()
        forward.append(copy)
    for o in range(1, n_tile):
        to_tiles[o - 1].wait_recv()
        total = total + scal_b_in[o - 1]
    sums = jnp.sum(total, axis=1, keepdims=True)
    factor = lax.rsqrt(sums[0:1] / (n_tile * ROWS * INPUTS) + guard_eps)
    loss_ref[...] = jnp.broadcast_to((sums[1:2] + sums[2:3]) / batch, loss_ref.shape)
    for copy in forward:
        copy.wait_recv()
    out_ref[...] = (-(gathered[...].astype(F32) * factor)).astype(BF16)

    for copies in (
        x_left, x_above, x_relay, fold_corner, fold_right, fold_below, e_left, e_above, e_relay,
        swap, scatter, to_dp, spread_out, forward, to_tiles,
    ):
        for copy in copies:
            copy.wait_send()


def local(n_dp, n_tile, side, frames, weights, connect):
    n_chip = n_dp // 2
    batch = frames.shape[-1] * n_dp
    dma = pltpu.SemaphoreType.DMA
    vmem = pl.BlockSpec(memory_space=pltpu.VMEM)
    tile = (3, PX, PX, 128)
    scratch = [
        pltpu.VMEM((WIDE, BAND), BF16),
        pltpu.VMEM((128, WIDE), BF16),
        pltpu.VMEM((ROWS, BAND), BF16),
        pltpu.VMEM((GROUPS, BAND, 128), BF16),
        pltpu.VMEM((96, 32, 128), BF16),
        pltpu.VMEM((96, 32, 128), BF16),
        pltpu.VMEM((ROWS, 128), F32),
        pltpu.VMEM((ROWS, 128), BF16),
        pltpu.VMEM((ROWS, 128), F32),
        pltpu.VMEM((96, 32, 128), F32),
        *[pltpu.VMEM(tile, BF16) for _ in range(6)],
        pltpu.VMEM((ROWS, BAND), F32),
        pltpu.VMEM((128, BAND), BF16),
        pltpu.VMEM((ROWS, WIDE), BF16),
        pltpu.VMEM((2, 128, WIDE), BF16),
        pltpu.VMEM((n_chip, ROWS // n_dp, WIDE), BF16),
        pltpu.VMEM((n_chip - 1, ROWS // n_dp, WIDE), BF16),
        pltpu.VMEM((ROWS, WIDE), BF16),
        pltpu.VMEM((8, 8, 128), F32),
        pltpu.VMEM((8, 128), F32),
        pltpu.VMEM((n_dp - 1, 8, 128), F32),
        pltpu.VMEM((8, 128), F32),
        pltpu.VMEM((n_tile - 1, 8, 128), F32),
        *[dma((9,)) for _ in range(6)],
        dma((2,)), dma((2,)),
        dma((n_chip - 1,)), dma((n_chip - 1,)),
        dma((n_dp - 1,)), dma((n_dp - 1,)),
        dma((n_chip - 1,)), dma((n_chip - 1,)),
        dma((n_chip,)), dma((n_chip,)),
        dma((n_tile - 1,)), dma((n_tile - 1,)),
    ]
    update, loss = pl.pallas_call(
        functools.partial(kernel, n_dp, n_tile, batch, side),
        out_shape=(
            jax.ShapeDtypeStruct((ROWS, WIDE), BF16),
            jax.ShapeDtypeStruct((8, 128), F32),
        ),
        in_specs=[vmem] * 3,
        out_specs=(vmem, vmem),
        scratch_shapes=scratch,
        compiler_params=pltpu.CompilerParams(
            collective_id=0, has_side_effects=True, vmem_limit_bytes=48 * 1024 * 1024
        ),
    )(frames[0], weights[0], connect[0])
    return update[:, :INPUTS].reshape(1, POS, MAPS, INPUTS), loss[0, 0]


def solution(mesh):
    n_dp, n_tile = mesh.shape["dp"], mesh.shape["tile"]
    side = int(round(n_tile ** 0.5))
    in_specs = (P("tile", None, None, None, "dp"), P("tile", None, None, None), P("tile", None, None, None))
    out_specs = (P("tile", None, None, None), P())
    return jax.shard_map(
        functools.partial(local, n_dp, n_tile, side), mesh=mesh, in_specs=in_specs, out_specs=out_specs, check_vma=False
    )
```

```python
import functools

import jax
import jax.numpy as jnp
from jax import lax
from jax.experimental import pallas as pl
from jax.experimental.pallas import tpu as pltpu
from jax.sharding import PartitionSpec as P

FIELD = 18
MAPS = 8
INPUTS = 972
POS = 64
PX = 16
BLOCK = 640
BAND = 3 * BLOCK
ROWS = POS * MAPS
WIDE = 1024
GROUPS = 4
MESH = pl.DeviceIdType.MESH
F32 = jnp.float32
BF16 = jnp.bfloat16

smooth_eps = 0.01
guard_eps = 1e-06


def dot(a, b):
    return lax.dot_general(a, b, (((1,), (0,)), ((), ())), preferred_element_type=F32)


def dot_nt(a, b):
    return lax.dot_general(a, b, (((1,), (1,)), ((), ())), preferred_element_type=F32)


def kernel(
    n_dp, n_tile, batch, side,
    frames_ref, w_ref, conn_ref,
    out_ref, loss_ref,
    w_in, opened, place, wpad, band, band_t, xext, eext, coded, coded_b, dec,
    right_src, right_in, corner_src, corner_in, below_src, below_in,
    gband, gsend, rs_in, rs_half, rs_parts, gathered,
    squares, scal, scal_in,
    in_sem, tok,
    x_send, x_recv, f_send, f_recv, e_send, e_recv,
    rs1_send, rs1_recv, rs2_send, rs2_recv, ag_send, ag_recv, fw_send, fw_recv, s_send, s_recv,
):
    d = lax.axis_index("dp")
    t = lax.axis_index("tile")
    n_chip = n_dp // 2
    core = lax.rem(d, 2)
    chip = lax.div(d, 2)
    left = (d, lax.rem(t + n_tile - 1, n_tile))
    right = (d, lax.rem(t + 1, n_tile))
    above = (d, lax.rem(t + n_tile - side, n_tile))
    below = (d, lax.rem(t + side, n_tile))
    sibling = (d + 1 - 2 * core, t)

    def at_chip(k):
        return (2 * k + core, t)

    flips = []
    bit = 1
    while bit < n_chip:
        flips.append(at_chip(chip + bit - 2 * bit * lax.rem(lax.div(chip, bit), 2)))
        bit *= 2

    barrier = pltpu.get_barrier_semaphore()
    greeted = [right, below, sibling, *flips]
    for device in greeted:
        pl.semaphore_signal(barrier, inc=1, device_id=device, device_id_type=MESH)
    own_in = pltpu.make_async_copy(frames_ref, xext.at[:, pl.ds(0, PX), pl.ds(0, PX)], in_sem.at[0])
    own_in.start()
    weights_in = pltpu.make_async_copy(w_ref, w_in, in_sem.at[1])
    weights_in.start()
    pl.semaphore_wait(barrier, len(greeted))

    sent = []

    def remote(src, dst, send, recv, device):
        return pltpu.make_async_remote_copy(
            src_ref=src, dst_ref=dst, send_sem=send, recv_sem=recv, device_id=device, device_id_type=MESH
        )

    def start(copy):
        copy.start()
        sent.append(copy)

    def quarter(ext, low, far, q):
        return ext.at[:, pl.ds(PX * low + 4 * q, 4), pl.ds(PX * far, PX)]

    def halo(own, ext, send, recv):
        to_left = [remote(own(q), quarter(ext, 0, 1, q), send.at[q], recv.at[q], left) for q in range(4)]
        to_above = [remote(own(q), quarter(ext, 1, 0, q), send.at[4 + q], recv.at[4 + q], above) for q in range(4)]
        relay = [
            remote(quarter(ext, 1, 0, q), quarter(ext, 1, 1, q), send.at[8 + q], recv.at[8 + q], left)
            for q in range(4)
        ]
        return to_left, to_above, relay

    x_left, x_above, x_relay = halo(lambda q: frames_ref.at[:, pl.ds(4 * q, 4)], xext, x_send, x_recv)
    start(x_above[0])
    for q in range(4):
        start(x_left[q])
    for q in range(1, 4):
        start(x_above[q])
    for device in flips:
        pl.semaphore_signal(tok.at[0], inc=1, device_id=device, device_id_type=MESH)

    lane = lax.broadcasted_iota(jnp.int32, (1, BAND), 1)
    chan = jnp.where(lane >= BLOCK, 1, 0) + jnp.where(lane >= 2 * BLOCK, 1, 0)
    spot = lane - BLOCK * chan
    prow = spot >> 5
    pcol = spot & 31
    source = jnp.where((pcol < FIELD) & (prow < FIELD), FIELD * FIELD * chan + FIELD * prow + pcol, -1)

    @pl.loop(0, WIDE // 32)
    def _(b):
        number = lax.broadcasted_iota(jnp.int32, (32, BAND), 0) + b * 32
        place[pl.ds(b * 32, 32), :] = jnp.where(number == source, 1.0, 0.0).astype(BF16)

    wpad[:, pl.ds(896, 128)] = jnp.zeros((128, 128), BF16)
    position = lax.broadcasted_iota(jnp.int32, (128, POS), 0) >> 3
    which = lax.broadcasted_iota(jnp.int32, (128, POS), 1)
    spans = ((0, 384), (256, 768), (640, 1024))
    weights_in.wait()

    @pl.loop(0, GROUPS)
    def _(g):
        rows = pl.ds(g * 128, 128)
        wpad[:, pl.ds(0, INPUTS)] = w_in[pl.ds(g * 16, 16)].astype(F32).reshape(128, INPUTS).astype(BF16)
        for c in range(3):
            maps = conn_ref[c].astype(F32)
            tall = jnp.concatenate([maps] * 16, axis=0)
            picked = jnp.where(which == position + g * 16, tall, 0.0)
            opened[c, rows] = jnp.broadcast_to(jnp.sum(picked, axis=1, keepdims=True), (128, 128))
            lanes = pl.ds(c * BLOCK, BLOCK)
            lo, hi = spans[c]
            spread = dot(wpad[:, lo:hi], place[lo:hi, lanes]) * opened[c, rows][:, 0:1]
            rolled = []
            for p in range(16):
                shift = 64 * (p // 8) + 2 * (p % 8)
                part = spread[p * 8 : p * 8 + 8]
                rolled.append(pltpu.roll(part, shift, 1) if shift else part)
            whole = jnp.concatenate(rolled, axis=0)
            band[rows, lanes] = whole.astype(BF16)
            band_t[g, lanes, :] = whole.T.astype(BF16)

    pl.semaphore_wait(tok.at[0], len(flips))
    for device in flips:
        pl.semaphore_signal(tok.at[1], inc=1, device_id=device, device_id_type=MESH)
    dec[...] = jnp.zeros(dec.shape, F32)
    squares[3:] = jnp.zeros((5, 8, 128), F32)
    own_in.wait()

    def strip(ext, g):
        return ext[:, pl.ds(4 * g, 20)].reshape(BAND, 128)

    fold_right = [
        remote(right_src.at[q], right_in.at[q], f_send.at[q], f_recv.at[q], right) for q in range(4)
    ]
    fold_corner = [
        remote(corner_src.at[q], corner_in.at[q], f_send.at[4 + q], f_recv.at[4 + q], right) for q in range(4)
    ]
    fold_below = [
        remote(below_src.at[q], below_in.at[q], f_send.at[8 + q], f_recv.at[8 + q], below) for q in range(4)
    ]
    for g in range(4):
        x_above[g].wait_recv()
        start(x_relay[g])
    for g in range(4):
        x_left[g].wait_recv()
    for g in range(4):
        x_relay[g].wait_recv()
        rows = pl.ds(g * 128, 128)
        value = dot(band[rows, :], strip(xext, g))
        rounded = value.astype(BF16)
        coded[rows] = value
        coded_b[rows] = rounded
        dec[:, pl.ds(4 * g, 20)] += dot(band_t[g], rounded).reshape(3, 20, 32, 128)
        if g < 3:
            right_src[g] = dec[:, pl.ds(4 * g, 4), pl.ds(PX, PX)].astype(BF16)
            start(fold_right[g])
    for q in range(4):
        corner_src[q] = dec[:, pl.ds(PX + 4 * q, 4), pl.ds(PX, PX)].astype(BF16)
        start(fold_corner[q])
    right_src[3] = dec[:, pl.ds(12, 4), pl.ds(PX, PX)].astype(BF16)
    start(fold_right[3])
    for q in range(4):
        fold_corner[q].wait_recv()
        summed = dec[:, pl.ds(PX + 4 * q, 4), pl.ds(0, PX)] + corner_in[q].astype(F32)
        below_src[q] = summed.astype(BF16)
        start(fold_below[q])

    value = coded[...]
    penalty = jnp.sqrt(smooth_eps + value * value)
    squares[2] = jnp.sum(penalty.reshape(ROWS // 8, 8, 128), axis=0)
    pl.semaphore_wait(tok.at[1], len(flips))

    e_left, e_above, e_relay = halo(lambda q: quarter(eext, 0, 0, q), eext, e_send, e_recv)
    error_sq = jnp.zeros((16, 128), F32)
    for q in range(4):
        fold_right[q].wait_recv()
        fold_below[q].wait_recv()
        own = (slice(None), pl.ds(4 * q, 4), pl.ds(0, PX))
        rebuilt = dec[own] + right_in[q].astype(F32) + below_in[q].astype(F32)
        error = rebuilt - xext[own].astype(F32)
        error_sq = error_sq + jnp.sum(error * error, axis=(0, 1))
        eext[own] = error.astype(BF16)
        start(e_above[q])
        start(e_left[q])
        if q > 0:
            e_above[q - 1].wait_recv()
            start(e_relay[q - 1])
    e_above[3].wait_recv()
    start(e_relay[3])
    squares[1] = error_sq[:8] + error_sq[8:]
    for q in range(4):
        e_left[q].wait_recv()

    def finish(g):
        rows = pl.ds(g * 128, 128)
        errors = strip(eext, g)
        value = coded[rows]
        enc = dot(band[rows, :], errors)
        coef = (2.0 * enc + value * lax.rsqrt(smooth_eps + value * value)).astype(BF16)
        both = jnp.concatenate([coded_b[rows] * 2, coef], axis=1)
        parts = []
        for c in range(3):
            lanes = slice(c * BLOCK, (c + 1) * BLOCK)
            patch = jnp.concatenate(
                [ext[c, pl.ds(4 * g, 20)].reshape(BLOCK, 128) for ext in (eext, xext)], axis=1
            )
            whole = dot_nt(both, patch) * opened[c, rows][:, 0:1]
            rolled = []
            for p in range(16):
                shift = 64 * (p // 8) + 2 * (p % 8)
                part = whole[p * 8 : p * 8 + 8]
                rolled.append(pltpu.roll(part, BLOCK - shift, 1) if shift else part)
            gband[...] = jnp.concatenate(rolled, axis=0).astype(BF16)
            lo, hi = spans[c]
            parts.append(dot_nt(gband[...], place[lo:hi, lanes]))
        first, middle, last = parts
        gsend[g, :, 0:256] = first[:, :256].astype(BF16)
        gsend[g, :, 256:384] = (first[:, 256:] + middle[:, :128]).astype(BF16)
        gsend[g, :, 384:640] = middle[:, 128:384].astype(BF16)
        gsend[g, :, 640:768] = (middle[:, 384:] + last[:, :128]).astype(BF16)
        gsend[g, :, 768:1024] = last[:, 128:].astype(BF16)

    def half_of(k):
        return pl.ds(pl.multiple_of(k * 64, 64), 64)

    def lanes_of(k):
        return pl.ds(pl.multiple_of(k * 128, 128), 128)

    swap = [
        remote(gsend.at[g, half_of(1 - core)], rs_in.at[g], rs1_send.at[g], rs1_recv.at[g], sibling)
        for g in range(4)
    ]
    scatter = []

    def combine(batch_no):
        for g in (2 * batch_no, 2 * batch_no + 1):
            swap[g].wait_recv()
            rs_half[g] = (gsend[g, half_of(core)].astype(F32) + rs_in[g].astype(F32)).astype(BF16)
        for o in range(1, n_chip):
            to = lax.rem(chip + o, n_chip)
            n = batch_no * (n_chip - 1) + o - 1
            copy = remote(
                rs_half.at[pl.ds(2 * batch_no, 2), :, lanes_of(to)],
                rs_parts.at[o - 1, pl.ds(2 * batch_no, 2)],
                rs2_send.at[n], rs2_recv.at[n], at_chip(to),
            )
            start(copy)
            scatter.append(copy)

    for g in range(4):
        e_relay[g].wait_recv()
        finish(g)
        start(swap[g])
        if g == 2:
            combine(0)
    combine(1)

    share = rs_half[:, :, lanes_of(chip)].astype(F32)
    for o in range(1, n_chip):
        scatter[o - 1].wait_recv()
        scatter[n_chip - 1 + o - 1].wait_recv()
        share = share + rs_parts[o - 1].astype(F32)

    def place_of(k):
        return gathered.at[:, core, :, lanes_of(k)]

    gathered[:, core, :, lanes_of(chip)] = share.astype(BF16)
    squares[0] = jnp.sum((share * share).reshape(32, 8, 128), axis=0)

    total = jnp.sum(squares[...], axis=1)
    scal[0] = total

    def exchange(stage, targets, first):
        copies = []
        for n, device in enumerate(targets):
            copy = remote(
                scal.at[stage], scal_in.at[first + n], s_send.at[first + n], s_recv.at[first + n], device
            )
            start(copy)
            copies.append(copy)
        return copies

    def collect(total, copies, first):
        for n, copy in enumerate(copies):
            copy.wait_recv()
            total = total + scal_in[first + n]
        return total

    rounds = [
        [at_chip(lax.rem(chip + o, n_chip)) for o in range(1, n_chip)],
        [sibling],
        [(d, lax.rem(t + side * o, n_tile)) for o in range(1, n_tile // side)],
        [(d, t - lax.rem(t, side) + lax.rem(t + o, side)) for o in range(1, side)],
    ]
    copies = exchange(0, rounds[0], 0)
    own_share = place_of(chip)
    spread_out = []
    for o in range(1, n_chip):
        to = lax.rem(chip + o, n_chip)
        copy = remote(own_share, own_share, ag_send.at[o - 1], ag_recv.at[o - 1], at_chip(to))
        start(copy)
        spread_out.append(copy)
    forward = [remote(own_share, own_share, fw_send.at[0], fw_recv.at[0], sibling)]
    start(forward[0])
    first = 0
    for stage in range(1, 4):
        total = collect(total, copies, first)
        first += len(copies)
        scal[stage] = total
        copies = exchange(stage, rounds[stage], first)
    for o in range(1, n_chip):
        origin = lax.rem(chip + n_chip - o, n_chip)
        arrived = place_of(origin)
        spread_out[o - 1].wait_recv()
        copy = remote(arrived, arrived, fw_send.at[o], fw_recv.at[o], sibling)
        start(copy)
        forward.append(copy)
    total = collect(total, copies, first)
    sums = jnp.sum(total, axis=1, keepdims=True)
    factor = lax.rsqrt(sums[0:1] / (n_tile * ROWS * INPUTS) + guard_eps)
    loss_ref[...] = jnp.broadcast_to((sums[1:2] + sums[2:3]) / batch, loss_ref.shape)
    for copy in forward:
        copy.wait_recv()
    out_ref[...] = (-(gathered[...].reshape(ROWS, WIDE).astype(F32) * factor)).astype(BF16)
    for copy in sent:
        copy.wait_send()


def local(n_dp, n_tile, side, frames, weights, connect):
    n_chip = n_dp // 2
    batch = frames.shape[-1] * n_dp
    dma = pltpu.SemaphoreType.DMA
    vmem = pl.BlockSpec(memory_space=pltpu.VMEM)
    hbm = pl.BlockSpec(memory_space=pltpu.HBM)
    n_small = n_chip - 1 + 1 + n_tile // side - 1 + side - 1
    scratch = [
        pltpu.VMEM((POS, MAPS, INPUTS), BF16),
        pltpu.VMEM((3, ROWS, 128), F32),
        pltpu.VMEM((WIDE, BAND), BF16),
        pltpu.VMEM((128, WIDE), BF16),
        pltpu.VMEM((ROWS, BAND), BF16),
        pltpu.VMEM((GROUPS, BAND, 128), BF16),
        pltpu.VMEM((3, 32, 32, 128), BF16),
        pltpu.VMEM((3, 32, 32, 128), BF16),
        pltpu.VMEM((ROWS, 128), F32),
        pltpu.VMEM((ROWS, 128), BF16),
        pltpu.VMEM((3, 32, 32, 128), F32),
        *[pltpu.VMEM((4, 3, 4, PX, 128), BF16) for _ in range(6)],
        pltpu.VMEM((128, BLOCK), BF16),
        pltpu.VMEM((GROUPS, 128, WIDE), BF16),
        pltpu.VMEM((GROUPS, 64, WIDE), BF16),
        pltpu.VMEM((GROUPS, 64, WIDE), BF16),
        pltpu.VMEM((n_chip - 1, GROUPS, 64, 128), BF16),
        pltpu.VMEM((GROUPS, 2, 64, WIDE), BF16),
        pltpu.VMEM((8, 8, 128), F32),
        pltpu.VMEM((4, 8, 128), F32),
        pltpu.VMEM((n_small, 8, 128), F32),
        dma((2,)),
        pltpu.SemaphoreType.REGULAR((2,)),
        *[dma((12,)) for _ in range(6)],
        dma((4,)), dma((4,)),
        dma((2 * (n_chip - 1),)), dma((2 * (n_chip - 1),)),
        dma((n_chip - 1,)), dma((n_chip - 1,)),
        dma((n_chip,)), dma((n_chip,)),
        dma((n_small,)), dma((n_small,)),
    ]
    update, loss = pl.pallas_call(
        functools.partial(kernel, n_dp, n_tile, batch, side),
        out_shape=(
            jax.ShapeDtypeStruct((ROWS, WIDE), BF16),
            jax.ShapeDtypeStruct((8, 128), F32),
        ),
        in_specs=[hbm, hbm, vmem],
        out_specs=(vmem, vmem),
        scratch_shapes=scratch,
        compiler_params=pltpu.CompilerParams(
            collective_id=0, has_side_effects=True, vmem_limit_bytes=63 * 1024 * 1024
        ),
    )(frames[0], weights[0], jnp.transpose(connect[0], (2, 1, 0)))
    return update[:, :INPUTS].reshape(1, POS, MAPS, INPUTS), loss[0, 0]


def solution(mesh):
    n_dp, n_tile = mesh.shape["dp"], mesh.shape["tile"]
    side = int(round(n_tile ** 0.5))
    in_specs = (P("tile", None, None, None, "dp"), P("tile", None, None, None), P("tile", None, None, None))
    out_specs = (P("tile", None, None, None), P())
    return jax.shard_map(
        functools.partial(local, n_dp, n_tile, side), mesh=mesh, in_specs=in_specs, out_specs=out_specs, check_vma=False
    )
```

```python
import functools

import jax
import jax.numpy as jnp
from jax import lax
from jax.experimental import pallas as pl
from jax.experimental.pallas import tpu as pltpu
from jax.sharding import PartitionSpec as P

FIELD = 18
MAPS = 8
INPUTS = 972
POS = 64
PX = 16
BLOCK = 640
BAND = 3 * BLOCK
ROWS = POS * MAPS
WIDE = 1024
GROUPS = 4
MESH = pl.DeviceIdType.MESH
F32 = jnp.float32
BF16 = jnp.bfloat16

smooth_eps = 0.01
guard_eps = 1e-06


def dot(a, b):
    return lax.dot_general(a, b, (((1,), (0,)), ((), ())), preferred_element_type=F32)


def dot_nt(a, b):
    return lax.dot_general(a, b, (((1,), (1,)), ((), ())), preferred_element_type=F32)


def kernel(
    n_dp, n_tile, batch, side,
    frames_ref, w_ref, conn_ref,
    out_ref, loss_ref,
    w_in, opened, place, wpad, band, band_t, xext, eext, coded, coded_b, dec,
    right_src, right_in, corner_src, corner_in, below_src, below_in,
    x_hold, e_hold, gband, gsend, rs_in, rs_half, rs_parts, gathered,
    squares, scal, scal_in,
    in_sem, tok,
    x_send, x_recv, f_send, f_recv, e_send, e_recv,
    rs1_send, rs1_recv, rs2_send, rs2_recv, ag_send, ag_recv, fw_send, fw_recv, s_send, s_recv,
):
    d = lax.axis_index("dp")
    t = lax.axis_index("tile")
    n_chip = n_dp // 2
    core = lax.rem(d, 2)
    chip = lax.div(d, 2)
    left = (d, lax.rem(t + n_tile - 1, n_tile))
    right = (d, lax.rem(t + 1, n_tile))
    above = (d, lax.rem(t + n_tile - side, n_tile))
    below = (d, lax.rem(t + side, n_tile))
    sibling = (d + 1 - 2 * core, t)

    def at_chip(k):
        return (2 * k + core, t)

    flips = []
    bit = 1
    while bit < n_chip:
        flips.append(at_chip(chip + bit - 2 * bit * lax.rem(lax.div(chip, bit), 2)))
        bit *= 2

    barrier = pltpu.get_barrier_semaphore()
    ahead = (d, lax.rem(t + 2, n_tile))
    behind = (d, lax.rem(t + n_tile - 2, n_tile))
    odd = lax.rem(t, 2)
    greeted = [right, below, left, ahead, sibling, *flips]
    for device in greeted:
        pl.semaphore_signal(barrier, inc=1, device_id=device, device_id_type=MESH)
    own_in = pltpu.make_async_copy(frames_ref, xext.at[:, pl.ds(0, PX), pl.ds(0, PX)], in_sem.at[0])
    own_in.start()
    weights_in = pltpu.make_async_copy(w_ref, w_in, in_sem.at[1])
    weights_in.start()
    pl.semaphore_wait(barrier, len(greeted))

    sent = []

    def remote(src, dst, send, recv, device):
        return pltpu.make_async_remote_copy(
            src_ref=src, dst_ref=dst, send_sem=send, recv_sem=recv, device_id=device, device_id_type=MESH
        )

    def start(copy, parity=None):
        if parity is None:
            copy.start()
        else:
            pl.when(odd == parity)(copy.start)
        sent.append((copy, parity))

    def start_left(direct, detour):
        start(direct, 1)
        start(detour, 0)

    def pass_on(arriving, onward):
        @pl.when(odd == 1)
        def _():
            arriving.wait_recv()
            onward.start()

        sent.append((onward, 1))

    def quarter(ext, low, far, q):
        return ext.at[:, pl.ds(PX * low + 4 * q, 4), pl.ds(PX * far, PX)]

    def halo(own, ext, hold, send, recv):
        to_left = [remote(own(q), quarter(ext, 0, 1, q), send.at[q], recv.at[q], left) for q in range(4)]
        to_above = [remote(own(q), quarter(ext, 1, 0, q), send.at[4 + q], recv.at[4 + q], above) for q in range(4)]
        relay = [
            remote(quarter(ext, 1, 0, q), quarter(ext, 1, 1, q), send.at[8 + q], recv.at[8 + q], left)
            for q in range(4)
        ]
        detour = [remote(own(q), hold.at[q], send.at[12 + q], recv.at[12 + q], right) for q in range(4)]
        onward = [remote(hold.at[q], quarter(ext, 0, 1, q), send.at[16 + q], recv.at[q], behind) for q in range(4)]
        return to_left, to_above, relay, detour, onward

    x_left, x_above, x_relay, x_detour, x_onward = halo(
        lambda q: frames_ref.at[:, pl.ds(4 * q, 4)], xext, x_hold, x_send, x_recv
    )
    for q in range(4):
        start(x_above[q])
    for q in range(4):
        start_left(x_left[q], x_detour[q])
    for device in flips:
        pl.semaphore_signal(tok.at[0], inc=1, device_id=device, device_id_type=MESH)

    lane = lax.broadcasted_iota(jnp.int32, (1, BAND), 1)
    chan = jnp.where(lane >= BLOCK, 1, 0) + jnp.where(lane >= 2 * BLOCK, 1, 0)
    spot = lane - BLOCK * chan
    prow = spot >> 5
    pcol = spot & 31
    source = jnp.where((pcol < FIELD) & (prow < FIELD), FIELD * FIELD * chan + FIELD * prow + pcol, -1)

    @pl.loop(0, WIDE // 32)
    def _(b):
        number = lax.broadcasted_iota(jnp.int32, (32, BAND), 0) + b * 32
        place[pl.ds(b * 32, 32), :] = jnp.where(number == source, 1.0, 0.0).astype(BF16)

    wpad[:, pl.ds(896, 128)] = jnp.zeros((128, 128), BF16)
    position = lax.broadcasted_iota(jnp.int32, (128, POS), 0) >> 3
    which = lax.broadcasted_iota(jnp.int32, (128, POS), 1)
    spans = ((0, 384), (256, 768), (640, 1024))
    weights_in.wait()

    def prepare(g):
        rows = pl.ds(g * 128, 128)
        wpad[:, pl.ds(0, INPUTS)] = w_in[pl.ds(g * 16, 16)].astype(F32).reshape(128, INPUTS).astype(BF16)
        for c in range(3):
            maps = conn_ref[c].astype(F32)
            tall = jnp.concatenate([maps] * 16, axis=0)
            picked = jnp.where(which == position + g * 16, tall, 0.0)
            opened[c, rows] = jnp.broadcast_to(jnp.sum(picked, axis=1, keepdims=True), (128, 128))
            lanes = pl.ds(c * BLOCK, BLOCK)
            lo, hi = spans[c]
            spread = dot(wpad[:, lo:hi], place[lo:hi, lanes]) * opened[c, rows][:, 0:1]
            rolled = []
            for p in range(16):
                shift = 64 * (p // 8) + 2 * (p % 8)
                part = spread[p * 8 : p * 8 + 8]
                rolled.append(pltpu.roll(part, shift, 1) if shift else part)
            whole = jnp.concatenate(rolled, axis=0)
            band[rows, lanes] = whole.astype(BF16)
            band_t[g, lanes, :] = whole.T.astype(BF16)

    prepare(0)
    for g in range(4):
        x_above[g].wait_recv()
        start(x_relay[g])
        if g < 3:
            prepare(g + 1)
        pass_on(x_detour[g], x_onward[g])
    pl.semaphore_wait(tok.at[0], len(flips))
    for device in flips:
        pl.semaphore_signal(tok.at[1], inc=1, device_id=device, device_id_type=MESH)
    dec[...] = jnp.zeros(dec.shape, F32)
    squares[3:] = jnp.zeros((5, 8, 128), F32)
    own_in.wait()

    def strip(ext, g):
        return ext[:, pl.ds(4 * g, 20)].reshape(BAND, 128)

    fold_right = [
        remote(right_src.at[q], right_in.at[q], f_send.at[q], f_recv.at[q], right) for q in range(4)
    ]
    fold_corner = [
        remote(corner_src.at[q], corner_in.at[q], f_send.at[4 + q], f_recv.at[4 + q], right) for q in range(4)
    ]
    fold_below = [
        remote(below_src.at[q], below_in.at[q], f_send.at[8 + q], f_recv.at[8 + q], below) for q in range(4)
    ]
    for g in range(4):
        x_left[g].wait_recv()
    for g in range(4):
        x_relay[g].wait_recv()
        rows = pl.ds(g * 128, 128)
        value = dot(band[rows, :], strip(xext, g))
        rounded = value.astype(BF16)
        coded[rows] = value
        coded_b[rows] = rounded
        dec[:, pl.ds(4 * g, 20)] += dot(band_t[g], rounded).reshape(3, 20, 32, 128)
        if g < 3:
            right_src[g] = dec[:, pl.ds(4 * g, 4), pl.ds(PX, PX)].astype(BF16)
            start(fold_right[g])
    for q in range(4):
        corner_src[q] = dec[:, pl.ds(PX + 4 * q, 4), pl.ds(PX, PX)].astype(BF16)
        start(fold_corner[q])
    right_src[3] = dec[:, pl.ds(12, 4), pl.ds(PX, PX)].astype(BF16)
    start(fold_right[3])
    for q in range(4):
        fold_corner[q].wait_recv()
        summed = dec[:, pl.ds(PX + 4 * q, 4), pl.ds(0, PX)] + corner_in[q].astype(F32)
        below_src[q] = summed.astype(BF16)
        start(fold_below[q])

    value = coded[...]
    penalty = jnp.sqrt(smooth_eps + value * value)
    squares[2] = jnp.sum(penalty.reshape(ROWS // 8, 8, 128), axis=0)
    pl.semaphore_wait(tok.at[1], len(flips))

    e_left, e_above, e_relay, e_detour, e_onward = halo(
        lambda q: quarter(eext, 0, 0, q), eext, e_hold, e_send, e_recv
    )
    error_sq = jnp.zeros((16, 128), F32)
    for q in range(4):
        fold_right[q].wait_recv()
        fold_below[q].wait_recv()
        own = (slice(None), pl.ds(4 * q, 4), pl.ds(0, PX))
        rebuilt = dec[own] + right_in[q].astype(F32) + below_in[q].astype(F32)
        error = rebuilt - xext[own].astype(F32)
        error_sq = error_sq + jnp.sum(error * error, axis=(0, 1))
        eext[own] = error.astype(BF16)
        start(e_above[q])
        start_left(e_left[q], e_detour[q])
        if q > 0:
            pass_on(e_detour[q - 1], e_onward[q - 1])
            e_above[q - 1].wait_recv()
            start(e_relay[q - 1])
    pass_on(e_detour[3], e_onward[3])
    e_above[3].wait_recv()
    start(e_relay[3])
    squares[1] = error_sq[:8] + error_sq[8:]
    for q in range(4):
        e_left[q].wait_recv()

    def finish(g):
        rows = pl.ds(g * 128, 128)
        errors = strip(eext, g)
        value = coded[rows]
        enc = dot(band[rows, :], errors)
        coef = (2.0 * enc + value * lax.rsqrt(smooth_eps + value * value)).astype(BF16)
        both = jnp.concatenate([coded_b[rows] * 2, coef], axis=1)
        parts = []
        for c in range(3):
            lanes = slice(c * BLOCK, (c + 1) * BLOCK)
            patch = jnp.concatenate(
                [ext[c, pl.ds(4 * g, 20)].reshape(BLOCK, 128) for ext in (eext, xext)], axis=1
            )
            whole = dot_nt(both, patch) * opened[c, rows][:, 0:1]
            rolled = []
            for p in range(16):
                shift = 64 * (p // 8) + 2 * (p % 8)
                part = whole[p * 8 : p * 8 + 8]
                rolled.append(pltpu.roll(part, BLOCK - shift, 1) if shift else part)
            gband[...] = jnp.concatenate(rolled, axis=0).astype(BF16)
            lo, hi = spans[c]
            parts.append(dot_nt(gband[...], place[lo:hi, lanes]))
        first, middle, last = parts
        gsend[g, :, 0:256] = first[:, :256].astype(BF16)
        gsend[g, :, 256:384] = (first[:, 256:] + middle[:, :128]).astype(BF16)
        gsend[g, :, 384:640] = middle[:, 128:384].astype(BF16)
        gsend[g, :, 640:768] = (middle[:, 384:] + last[:, :128]).astype(BF16)
        gsend[g, :, 768:1024] = last[:, 128:].astype(BF16)

    def half_of(k):
        return pl.ds(pl.multiple_of(k * 64, 64), 64)

    def lanes_of(k):
        return pl.ds(pl.multiple_of(k * 128, 128), 128)

    swap = [
        remote(gsend.at[g, half_of(1 - core)], rs_in.at[g], rs1_send.at[g], rs1_recv.at[g], sibling)
        for g in range(4)
    ]
    scatter = []

    def combine(batch_no):
        for g in (2 * batch_no, 2 * batch_no + 1):
            swap[g].wait_recv()
            rs_half[g] = (gsend[g, half_of(core)].astype(F32) + rs_in[g].astype(F32)).astype(BF16)
        for o in range(1, n_chip):
            to = lax.rem(chip + o, n_chip)
            n = batch_no * (n_chip - 1) + o - 1
            copy = remote(
                rs_half.at[pl.ds(2 * batch_no, 2), :, lanes_of(to)],
                rs_parts.at[o - 1, pl.ds(2 * batch_no, 2)],
                rs2_send.at[n], rs2_recv.at[n], at_chip(to),
            )
            start(copy)
            scatter.append(copy)

    for g in range(4):
        e_relay[g].wait_recv()
        finish(g)
        start(swap[g])
        if g == 2:
            combine(0)
    combine(1)

    def place_of(batch_no, k):
        return gathered.at[pl.ds(2 * batch_no, 2), core, :, lanes_of(k)]

    spread_out = [[], []]
    forward = []

    def pass_to_sibling(batch_no, k, o):
        n = batch_no * n_chip + o
        block = place_of(batch_no, k)
        copy = remote(block, block, fw_send.at[n], fw_recv.at[n], sibling)
        start(copy)
        forward.append(copy)

    def gather(batch_no):
        block = place_of(batch_no, chip)
        for o in range(1, n_chip):
            n = batch_no * (n_chip - 1) + o - 1
            to = lax.rem(chip + o, n_chip)
            copy = remote(block, block, ag_send.at[n], ag_recv.at[n], at_chip(to))
            start(copy)
            spread_out[batch_no].append(copy)
        pass_to_sibling(batch_no, chip, 0)

    def hand_on(batch_no):
        for o in range(1, n_chip):
            spread_out[batch_no][o - 1].wait_recv()
            pass_to_sibling(batch_no, lax.rem(chip + n_chip - o, n_chip), o)

    def add_up(batch_no):
        pair = pl.ds(2 * batch_no, 2)
        share = rs_half[pair, :, lanes_of(chip)].astype(F32)
        for o in range(1, n_chip):
            scatter[batch_no * (n_chip - 1) + o - 1].wait_recv()
            share = share + rs_parts[o - 1, pair].astype(F32)
        gathered[pair, core, :, lanes_of(chip)] = share.astype(BF16)
        return jnp.sum((share * share).reshape(16, 8, 128), axis=0)

    square = add_up(0)
    gather(0)
    squares[0] = square + add_up(1)

    total = jnp.sum(squares[...], axis=1)
    scal[0] = total

    def exchange(stage, targets, first):
        copies = []
        for n, device in enumerate(targets):
            copy = remote(
                scal.at[stage], scal_in.at[first + n], s_send.at[first + n], s_recv.at[first + n], device
            )
            start(copy)
            copies.append(copy)
        return copies

    def collect(total, copies, first):
        for n, copy in enumerate(copies):
            copy.wait_recv()
            total = total + scal_in[first + n]
        return total

    rounds = [
        [at_chip(lax.rem(chip + o, n_chip)) for o in range(1, n_chip)],
        [
            (d + other * (1 - 2 * core), lax.rem(t + side * o, n_tile))
            for other in range(2) for o in range(n_tile // side) if other or o
        ],
        [(d, t - lax.rem(t, side) + lax.rem(t + o, side)) for o in range(1, side)],
    ]
    copies = exchange(0, rounds[0], 0)
    gather(1)
    hand_on(0)
    first = 0
    for stage in range(1, 3):
        total = collect(total, copies, first)
        first += len(copies)
        scal[stage] = total
        copies = exchange(stage, rounds[stage], first)
    hand_on(1)
    total = collect(total, copies, first)
    sums = jnp.sum(total, axis=1, keepdims=True)
    factor = lax.rsqrt(sums[0:1] / (n_tile * ROWS * INPUTS) + guard_eps)
    loss_ref[...] = jnp.broadcast_to((sums[1:2] + sums[2:3]) / batch, loss_ref.shape)
    for copy in forward:
        copy.wait_recv()
    out_ref[...] = (-(gathered[...].reshape(ROWS, WIDE).astype(F32) * factor)).astype(BF16)
    for copy, parity in sent:
        if parity is None:
            copy.wait_send()
        else:
            pl.when(odd == parity)(copy.wait_send)


def local(n_dp, n_tile, side, frames, weights, connect):
    n_chip = n_dp // 2
    batch = frames.shape[-1] * n_dp
    dma = pltpu.SemaphoreType.DMA
    vmem = pl.BlockSpec(memory_space=pltpu.VMEM)
    hbm = pl.BlockSpec(memory_space=pltpu.HBM)
    n_small = n_chip - 1 + 2 * (n_tile // side) - 1 + side - 1
    scratch = [
        pltpu.VMEM((POS, MAPS, INPUTS), BF16),
        pltpu.VMEM((3, ROWS, 128), F32),
        pltpu.VMEM((WIDE, BAND), BF16),
        pltpu.VMEM((128, WIDE), BF16),
        pltpu.VMEM((ROWS, BAND), BF16),
        pltpu.VMEM((GROUPS, BAND, 128), BF16),
        pltpu.VMEM((3, 32, 32, 128), BF16),
        pltpu.VMEM((3, 32, 32, 128), BF16),
        pltpu.VMEM((ROWS, 128), F32),
        pltpu.VMEM((ROWS, 128), BF16),
        pltpu.VMEM((3, 32, 32, 128), F32),
        *[pltpu.VMEM((4, 3, 4, PX, 128), BF16) for _ in range(6)],
        *[pltpu.VMEM((4, 3, 4, PX, 128), BF16) for _ in range(2)],
        pltpu.VMEM((128, BLOCK), BF16),
        pltpu.VMEM((GROUPS, 128, WIDE), BF16),
        pltpu.VMEM((GROUPS, 64, WIDE), BF16),
        pltpu.VMEM((GROUPS, 64, WIDE), BF16),
        pltpu.VMEM((n_chip - 1, GROUPS, 64, 128), BF16),
        pltpu.VMEM((GROUPS, 2, 64, WIDE), BF16),
        pltpu.VMEM((8, 8, 128), F32),
        pltpu.VMEM((4, 8, 128), F32),
        pltpu.VMEM((n_small, 8, 128), F32),
        dma((2,)),
        pltpu.SemaphoreType.REGULAR((2,)),
        *[dma((20,)) for _ in range(6)],
        dma((4,)), dma((4,)),
        dma((2 * (n_chip - 1),)), dma((2 * (n_chip - 1),)),
        dma((2 * (n_chip - 1),)), dma((2 * (n_chip - 1),)),
        dma((2 * n_chip,)), dma((2 * n_chip,)),
        dma((n_small,)), dma((n_small,)),
    ]
    update, loss = pl.pallas_call(
        functools.partial(kernel, n_dp, n_tile, batch, side),
        out_shape=(
            jax.ShapeDtypeStruct((ROWS, WIDE), BF16),
            jax.ShapeDtypeStruct((8, 128), F32),
        ),
        in_specs=[hbm, hbm, vmem],
        out_specs=(vmem, vmem),
        scratch_shapes=scratch,
        compiler_params=pltpu.CompilerParams(
            collective_id=0, has_side_effects=True, vmem_limit_bytes=54000 * 1024
        ),
    )(frames[0], weights[0], jnp.transpose(connect[0], (2, 1, 0)))
    return update[:, :INPUTS].reshape(1, POS, MAPS, INPUTS), loss[0, 0]


def solution(mesh):
    n_dp, n_tile = mesh.shape["dp"], mesh.shape["tile"]
    side = int(round(n_tile ** 0.5))
    in_specs = (P("tile", None, None, None, "dp"), P("tile", None, None, None), P("tile", None, None, None))
    out_specs = (P("tile", None, None, None), P())
    return jax.shard_map(
        functools.partial(local, n_dp, n_tile, side), mesh=mesh, in_specs=in_specs, out_specs=out_specs, check_vma=False
    )
```

```python
import functools

import jax
import jax.numpy as jnp
from jax import lax
from jax.experimental import pallas as pl
from jax.experimental.pallas import tpu as pltpu
from jax.sharding import PartitionSpec as P

FIELD = 18
MAPS = 8
INPUTS = 972
POS = 64
PX = 16
BLOCK = 640
BAND = 3 * BLOCK
ROWS = POS * MAPS
WIDE = 1024
GROUPS = 4
MESH = pl.DeviceIdType.MESH
F32 = jnp.float32
BF16 = jnp.bfloat16

smooth_eps = 0.01
guard_eps = 1e-06


def dot(a, b):
    return lax.dot_general(a, b, (((1,), (0,)), ((), ())), preferred_element_type=F32)


def dot_nt(a, b):
    return lax.dot_general(a, b, (((1,), (1,)), ((), ())), preferred_element_type=F32)


def kernel(
    n_dp, n_tile, batch, side,
    frames_ref, w_ref, conn_ref,
    out_ref, loss_ref,
    w_in, opened, place, wpad, band, band_t, xext, eext, coded, coded_b, dec,
    right_src, right_in, corner_src, corner_in, below_src, below_in,
    x_hold, e_hold, gband, gsend, rs_in, rs_half, rs_parts, gathered,
    squares, scal, scal_in,
    in_sem, tok,
    x_send, x_recv, f_send, f_recv, e_send, e_recv,
    rs1_send, rs1_recv, rs2_send, rs2_recv, ag_send, ag_recv, fw_send, fw_recv, s_send, s_recv,
):
    d = lax.axis_index("dp")
    t = lax.axis_index("tile")
    n_chip = n_dp // 2
    core = lax.rem(d, 2)
    chip = lax.div(d, 2)
    left = (d, lax.rem(t + n_tile - 1, n_tile))
    right = (d, lax.rem(t + 1, n_tile))
    above = (d, lax.rem(t + n_tile - side, n_tile))
    below = (d, lax.rem(t + side, n_tile))
    sibling = (d + 1 - 2 * core, t)

    def at_chip(k):
        return (2 * k + core, t)

    n_x = n_chip // 2
    x_at = lax.div(chip, 2)
    y_at = lax.rem(chip, 2)
    along_x = sorted(range(n_x), key=lambda o: -min(o, n_x - o))
    steps = [(dx, 1) for dx in along_x] + [(dx, 0) for dx in along_x if dx]

    def chip_to(step):
        return 2 * lax.rem(x_at + step[0], n_x) + lax.rem(y_at + step[1], 2)

    def chip_from(step):
        return 2 * lax.rem(x_at + n_x - step[0], n_x) + lax.rem(y_at + step[1], 2)

    flips = []
    bit = 1
    while bit < n_chip:
        flips.append(at_chip(chip + bit - 2 * bit * lax.rem(lax.div(chip, bit), 2)))
        bit *= 2

    barrier = pltpu.get_barrier_semaphore()
    ahead = (d, lax.rem(t + 2, n_tile))
    behind = (d, lax.rem(t + n_tile - 2, n_tile))
    odd = lax.rem(t, 2)
    greeted = [right, below, left, ahead, sibling, *flips]
    for device in greeted:
        pl.semaphore_signal(barrier, inc=1, device_id=device, device_id_type=MESH)
    own_in = pltpu.make_async_copy(frames_ref, xext.at[:, pl.ds(0, PX), pl.ds(0, PX)], in_sem.at[0])
    own_in.start()
    weights_in = pltpu.make_async_copy(w_ref, w_in, in_sem.at[1])
    weights_in.start()
    pl.semaphore_wait(barrier, len(greeted))

    sent = []

    def remote(src, dst, send, recv, device):
        return pltpu.make_async_remote_copy(
            src_ref=src, dst_ref=dst, send_sem=send, recv_sem=recv, device_id=device, device_id_type=MESH
        )

    def start(copy, parity=None):
        if parity is None:
            copy.start()
        else:
            pl.when(odd == parity)(copy.start)
        sent.append((copy, parity))

    def start_left(direct, detour):
        start(direct, 1)
        start(detour, 0)

    def pass_on(arriving, onward):
        @pl.when(odd == 1)
        def _():
            arriving.wait_recv()
            onward.start()

        sent.append((onward, 1))

    def quarter(ext, low, far, q):
        return ext.at[:, pl.ds(PX * low + 4 * q, 4), pl.ds(PX * far, PX)]

    def halo(own, ext, hold, send, recv):
        to_left = [remote(own(q), quarter(ext, 0, 1, q), send.at[q], recv.at[q], left) for q in range(4)]
        to_above = [remote(own(q), quarter(ext, 1, 0, q), send.at[4 + q], recv.at[4 + q], above) for q in range(4)]
        relay = [
            remote(quarter(ext, 1, 0, q), quarter(ext, 1, 1, q), send.at[8 + q], recv.at[8 + q], left)
            for q in range(4)
        ]
        detour = [remote(own(q), hold.at[q], send.at[12 + q], recv.at[12 + q], right) for q in range(4)]
        onward = [remote(hold.at[q], quarter(ext, 0, 1, q), send.at[16 + q], recv.at[q], behind) for q in range(4)]
        return to_left, to_above, relay, detour, onward

    x_left, x_above, x_relay, x_detour, x_onward = halo(
        lambda q: frames_ref.at[:, pl.ds(4 * q, 4)], xext, x_hold, x_send, x_recv
    )
    for q in range(4):
        start(x_above[q])
    for q in range(4):
        start_left(x_left[q], x_detour[q])
    for device in flips:
        pl.semaphore_signal(tok.at[0], inc=1, device_id=device, device_id_type=MESH)

    lane = lax.broadcasted_iota(jnp.int32, (1, BAND), 1)
    chan = jnp.where(lane >= BLOCK, 1, 0) + jnp.where(lane >= 2 * BLOCK, 1, 0)
    spot = lane - BLOCK * chan
    prow = spot >> 5
    pcol = spot & 31
    source = jnp.where((pcol < FIELD) & (prow < FIELD), FIELD * FIELD * chan + FIELD * prow + pcol, -1)

    @pl.loop(0, WIDE // 32)
    def _(b):
        number = lax.broadcasted_iota(jnp.int32, (32, BAND), 0) + b * 32
        place[pl.ds(b * 32, 32), :] = jnp.where(number == source, 1.0, 0.0).astype(BF16)

    wpad[:, pl.ds(896, 128)] = jnp.zeros((128, 128), BF16)
    position = lax.broadcasted_iota(jnp.int32, (128, POS), 0) >> 3
    which = lax.broadcasted_iota(jnp.int32, (128, POS), 1)
    spans = ((0, 384), (256, 768), (640, 1024))
    weights_in.wait()

    def prepare(g):
        rows = pl.ds(g * 128, 128)
        wpad[:, pl.ds(0, INPUTS)] = w_in[pl.ds(g * 16, 16)].astype(F32).reshape(128, INPUTS).astype(BF16)
        for c in range(3):
            maps = conn_ref[c].astype(F32)
            tall = jnp.concatenate([maps] * 16, axis=0)
            picked = jnp.where(which == position + g * 16, tall, 0.0)
            opened[c, rows] = jnp.broadcast_to(jnp.sum(picked, axis=1, keepdims=True), (128, 128))
            lanes = pl.ds(c * BLOCK, BLOCK)
            lo, hi = spans[c]
            spread = dot(wpad[:, lo:hi], place[lo:hi, lanes]) * opened[c, rows][:, 0:1]
            rolled = []
            for p in range(16):
                shift = 64 * (p // 8) + 2 * (p % 8)
                part = spread[p * 8 : p * 8 + 8]
                rolled.append(pltpu.roll(part, shift, 1) if shift else part)
            whole = jnp.concatenate(rolled, axis=0)
            band[rows, lanes] = whole.astype(BF16)
            band_t[g, lanes, :] = whole.T.astype(BF16)

    prepare(0)
    for g in range(4):
        x_above[g].wait_recv()
        start(x_relay[g])
        if g < 3:
            prepare(g + 1)
        pass_on(x_detour[g], x_onward[g])
    pl.semaphore_wait(tok.at[0], len(flips))
    for device in flips:
        pl.semaphore_signal(tok.at[1], inc=1, device_id=device, device_id_type=MESH)
    dec[...] = jnp.zeros(dec.shape, F32)
    squares[3:] = jnp.zeros((5, 8, 128), F32)
    own_in.wait()

    def strip(ext, g):
        return ext[:, pl.ds(4 * g, 20)].reshape(BAND, 128)

    fold_right = [
        remote(right_src.at[q], right_in.at[q], f_send.at[q], f_recv.at[q], right) for q in range(4)
    ]
    fold_corner = [
        remote(corner_src.at[q], corner_in.at[q], f_send.at[4 + q], f_recv.at[4 + q], right) for q in range(4)
    ]
    fold_below = [
        remote(below_src.at[q], below_in.at[q], f_send.at[8 + q], f_recv.at[8 + q], below) for q in range(4)
    ]
    for g in range(4):
        x_left[g].wait_recv()
    for g in range(4):
        x_relay[g].wait_recv()
        rows = pl.ds(g * 128, 128)
        value = dot(band[rows, :], strip(xext, g))
        rounded = value.astype(BF16)
        coded[rows] = value
        coded_b[rows] = rounded
        dec[:, pl.ds(4 * g, 20)] += dot(band_t[g], rounded).reshape(3, 20, 32, 128)
        if g < 3:
            right_src[g] = dec[:, pl.ds(4 * g, 4), pl.ds(PX, PX)].astype(BF16)
            start(fold_right[g])
    for q in range(4):
        corner_src[q] = dec[:, pl.ds(PX + 4 * q, 4), pl.ds(PX, PX)].astype(BF16)
        start(fold_corner[q])
    right_src[3] = dec[:, pl.ds(12, 4), pl.ds(PX, PX)].astype(BF16)
    start(fold_right[3])
    for q in range(4):
        fold_corner[q].wait_recv()
        summed = dec[:, pl.ds(PX + 4 * q, 4), pl.ds(0, PX)] + corner_in[q].astype(F32)
        below_src[q] = summed.astype(BF16)
        start(fold_below[q])

    value = coded[...]
    penalty = jnp.sqrt(smooth_eps + value * value)
    squares[2] = jnp.sum(penalty.reshape(ROWS // 8, 8, 128), axis=0)
    pl.semaphore_wait(tok.at[1], len(flips))

    e_left, e_above, e_relay, e_detour, e_onward = halo(
        lambda q: quarter(eext, 0, 0, q), eext, e_hold, e_send, e_recv
    )
    error_sq = jnp.zeros((16, 128), F32)
    for q in range(4):
        fold_right[q].wait_recv()
        fold_below[q].wait_recv()
        own = (slice(None), pl.ds(4 * q, 4), pl.ds(0, PX))
        rebuilt = dec[own] + right_in[q].astype(F32) + below_in[q].astype(F32)
        error = rebuilt - xext[own].astype(F32)
        error_sq = error_sq + jnp.sum(error * error, axis=(0, 1))
        eext[own] = error.astype(BF16)
        start(e_above[q])
        start_left(e_left[q], e_detour[q])
        if q > 0:
            pass_on(e_detour[q - 1], e_onward[q - 1])
            e_above[q - 1].wait_recv()
            start(e_relay[q - 1])
    pass_on(e_detour[3], e_onward[3])
    e_above[3].wait_recv()
    start(e_relay[3])
    squares[1] = error_sq[:8] + error_sq[8:]
    for q in range(4):
        e_left[q].wait_recv()

    def finish(g):
        rows = pl.ds(g * 128, 128)
        errors = strip(eext, g)
        value = coded[rows]
        enc = dot(band[rows, :], errors)
        coef = (2.0 * enc + value * lax.rsqrt(smooth_eps + value * value)).astype(BF16)
        both = jnp.concatenate([coded_b[rows] * 2, coef], axis=1)
        parts = []
        for c in range(3):
            lanes = slice(c * BLOCK, (c + 1) * BLOCK)
            patch = jnp.concatenate(
                [ext[c, pl.ds(4 * g, 20)].reshape(BLOCK, 128) for ext in (eext, xext)], axis=1
            )
            whole = dot_nt(both, patch) * opened[c, rows][:, 0:1]
            rolled = []
            for p in range(16):
                shift = 64 * (p // 8) + 2 * (p % 8)
                part = whole[p * 8 : p * 8 + 8]
                rolled.append(pltpu.roll(part, BLOCK - shift, 1) if shift else part)
            gband[...] = jnp.concatenate(rolled, axis=0).astype(BF16)
            lo, hi = spans[c]
            parts.append(dot_nt(gband[...], place[lo:hi, lanes]))
        first, middle, last = parts
        gsend[g, :, 0:256] = first[:, :256].astype(BF16)
        gsend[g, :, 256:384] = (first[:, 256:] + middle[:, :128]).astype(BF16)
        gsend[g, :, 384:640] = middle[:, 128:384].astype(BF16)
        gsend[g, :, 640:768] = (middle[:, 384:] + last[:, :128]).astype(BF16)
        gsend[g, :, 768:1024] = last[:, 128:].astype(BF16)

    def half_of(k):
        return pl.ds(pl.multiple_of(k * 64, 64), 64)

    def lanes_of(k):
        return pl.ds(pl.multiple_of(k * 128, 128), 128)

    swap = [
        remote(gsend.at[g, half_of(1 - core)], rs_in.at[g], rs1_send.at[g], rs1_recv.at[g], sibling)
        for g in range(4)
    ]
    scatter = []

    def combine(batch_no):
        for g in (2 * batch_no, 2 * batch_no + 1):
            swap[g].wait_recv()
            rs_half[g] = (gsend[g, half_of(core)].astype(F32) + rs_in[g].astype(F32)).astype(BF16)
        for o, step in enumerate(steps, 1):
            to = chip_to(step)
            n = batch_no * (n_chip - 1) + o - 1
            copy = remote(
                rs_half.at[pl.ds(2 * batch_no, 2), :, lanes_of(to)],
                rs_parts.at[o - 1, pl.ds(2 * batch_no, 2)],
                rs2_send.at[n], rs2_recv.at[n], at_chip(to),
            )
            start(copy)
            scatter.append(copy)

    for g in range(4):
        e_relay[g].wait_recv()
        finish(g)
        start(swap[g])
        if g == 2:
            combine(0)
    combine(1)

    def place_of(batch_no, k):
        return gathered.at[pl.ds(2 * batch_no, 2), core, :, lanes_of(k)]

    spread_out = [[], []]
    forward = []

    def pass_to_sibling(batch_no, k, o):
        n = batch_no * n_chip + o
        block = place_of(batch_no, k)
        copy = remote(block, block, fw_send.at[n], fw_recv.at[n], sibling)
        start(copy)
        forward.append(copy)

    def gather(batch_no):
        block = place_of(batch_no, chip)
        for o, step in enumerate(steps, 1):
            n = batch_no * (n_chip - 1) + o - 1
            to = chip_to(step)
            copy = remote(block, block, ag_send.at[n], ag_recv.at[n], at_chip(to))
            start(copy)
            spread_out[batch_no].append(copy)
        pass_to_sibling(batch_no, chip, 0)

    def hand_on(batch_no):
        for o in reversed(range(1, n_chip)):
            spread_out[batch_no][o - 1].wait_recv()
            pass_to_sibling(batch_no, chip_from(steps[o - 1]), o)

    def add_up(batch_no):
        pair = pl.ds(2 * batch_no, 2)
        share = rs_half[pair, :, lanes_of(chip)].astype(F32)
        for o in range(1, n_chip):
            scatter[batch_no * (n_chip - 1) + o - 1].wait_recv()
            share = share + rs_parts[o - 1, pair].astype(F32)
        gathered[pair, core, :, lanes_of(chip)] = share.astype(BF16)
        return jnp.sum((share * share).reshape(16, 8, 128), axis=0)

    square = add_up(0)
    gather(0)
    squares[0] = square + add_up(1)

    total = jnp.sum(squares[...], axis=1)
    scal[0] = total

    def exchange(stage, targets, first):
        copies = []
        for n, device in enumerate(targets):
            copy = remote(
                scal.at[stage], scal_in.at[first + n], s_send.at[first + n], s_recv.at[first + n], device
            )
            start(copy)
            copies.append(copy)
        return copies

    def collect(total, copies, first):
        for n, copy in enumerate(copies):
            copy.wait_recv()
            total = total + scal_in[first + n]
        return total

    rounds = [
        [(2 * chip_to(step) + lax.rem(core + o, 2), t) for step in steps for o in (1, 0)] + [sibling],
        [(d, lax.rem(t + o, n_tile)) for o in sorted(range(1, n_tile), key=lambda o: -min(o, n_tile - o))],
    ]
    copies = exchange(0, rounds[0], 0)
    gather(1)
    first = 0
    for stage in range(1, len(rounds)):
        total = collect(total, copies, first)
        first += len(copies)
        scal[stage] = total
        copies = exchange(stage, rounds[stage], first)
    hand_on(0)
    hand_on(1)
    total = collect(total, copies, first)
    sums = jnp.sum(total, axis=1, keepdims=True)
    factor = lax.rsqrt(sums[0:1] / (n_tile * ROWS * INPUTS) + guard_eps)
    loss_ref[...] = jnp.broadcast_to((sums[1:2] + sums[2:3]) / batch, loss_ref.shape)
    for copy in forward:
        copy.wait_recv()
    out_ref[...] = (-(gathered[...].reshape(ROWS, WIDE).astype(F32) * factor)).astype(BF16)
    for copy, parity in sent:
        if parity is None:
            copy.wait_send()
        else:
            pl.when(odd == parity)(copy.wait_send)


def local(n_dp, n_tile, side, frames, weights, connect):
    n_chip = n_dp // 2
    batch = frames.shape[-1] * n_dp
    dma = pltpu.SemaphoreType.DMA
    vmem = pl.BlockSpec(memory_space=pltpu.VMEM)
    hbm = pl.BlockSpec(memory_space=pltpu.HBM)
    n_small = n_dp + n_tile - 2
    scratch = [
        pltpu.VMEM((POS, MAPS, INPUTS), BF16),
        pltpu.VMEM((3, ROWS, 128), F32),
        pltpu.VMEM((WIDE, BAND), BF16),
        pltpu.VMEM((128, WIDE), BF16),
        pltpu.VMEM((ROWS, BAND), BF16),
        pltpu.VMEM((GROUPS, BAND, 128), BF16),
        pltpu.VMEM((3, 32, 32, 128), BF16),
        pltpu.VMEM((3, 32, 32, 128), BF16),
        pltpu.VMEM((ROWS, 128), F32),
        pltpu.VMEM((ROWS, 128), BF16),
        pltpu.VMEM((3, 32, 32, 128), F32),
        *[pltpu.VMEM((4, 3, 4, PX, 128), BF16) for _ in range(6)],
        *[pltpu.VMEM((4, 3, 4, PX, 128), BF16) for _ in range(2)],
        pltpu.VMEM((128, BLOCK), BF16),
        pltpu.VMEM((GROUPS, 128, WIDE), BF16),
        pltpu.VMEM((GROUPS, 64, WIDE), BF16),
        pltpu.VMEM((GROUPS, 64, WIDE), BF16),
        pltpu.VMEM((n_chip - 1, GROUPS, 64, 128), BF16),
        pltpu.VMEM((GROUPS, 2, 64, WIDE), BF16),
        pltpu.VMEM((8, 8, 128), F32),
        pltpu.VMEM((4, 8, 128), F32),
        pltpu.VMEM((n_small, 8, 128), F32),
        dma((2,)),
        pltpu.SemaphoreType.REGULAR((2,)),
        *[dma((20,)) for _ in range(6)],
        dma((4,)), dma((4,)),
        dma((2 * (n_chip - 1),)), dma((2 * (n_chip - 1),)),
        dma((2 * (n_chip - 1),)), dma((2 * (n_chip - 1),)),
        dma((2 * n_chip,)), dma((2 * n_chip,)),
        dma((n_small,)), dma((n_small,)),
    ]
    update, loss = pl.pallas_call(
        functools.partial(kernel, n_dp, n_tile, batch, side),
        out_shape=(
            jax.ShapeDtypeStruct((ROWS, WIDE), BF16),
            jax.ShapeDtypeStruct((8, 128), F32),
        ),
        in_specs=[hbm, hbm, vmem],
        out_specs=(vmem, vmem),
        scratch_shapes=scratch,
        compiler_params=pltpu.CompilerParams(
            collective_id=0, has_side_effects=True, vmem_limit_bytes=54000 * 1024
        ),
    )(frames[0], weights[0], jnp.transpose(connect[0], (2, 1, 0)))
    return update[:, :INPUTS].reshape(1, POS, MAPS, INPUTS), loss[0, 0]


def solution(mesh):
    n_dp, n_tile = mesh.shape["dp"], mesh.shape["tile"]
    side = int(round(n_tile ** 0.5))
    in_specs = (P("tile", None, None, None, "dp"), P("tile", None, None, None), P("tile", None, None, None))
    out_specs = (P("tile", None, None, None), P())
    return jax.shard_map(
        functools.partial(local, n_dp, n_tile, side), mesh=mesh, in_specs=in_specs, out_specs=out_specs, check_vma=False
    )
```

```python
import functools

import jax
import jax.numpy as jnp
from jax import lax
from jax.experimental import pallas as pl
from jax.experimental.pallas import tpu as pltpu
from jax.sharding import PartitionSpec as P

FIELD = 18
MAPS = 8
INPUTS = 972
POS = 64
PX = 16
BLOCK = 640
BAND = 3 * BLOCK
ROWS = POS * MAPS
WIDE = 1024
GROUPS = 4
MESH = pl.DeviceIdType.MESH
F32 = jnp.float32
BF16 = jnp.bfloat16

smooth_eps = 0.01
guard_eps = 1e-06


def dot(a, b):
    return lax.dot_general(a, b, (((1,), (0,)), ((), ())), preferred_element_type=F32)


def dot_nt(a, b):
    return lax.dot_general(a, b, (((1,), (1,)), ((), ())), preferred_element_type=F32)


def kernel(
    n_dp, n_tile, batch, side,
    frames_ref, w_ref, conn_ref,
    out_ref, loss_ref,
    w_in, opened, place, wpad, band, band_t, xext, eext, coded, coded_b, dec,
    right_src, right_in, corner_src, corner_in, below_src, below_in,
    x_hold, e_hold, gband, gsend, rs_in, rs_half, rs_parts, gathered,
    squares, scal, scal_in,
    in_sem, tok,
    x_send, x_recv, f_send, f_recv, e_send, e_recv,
    rs1_send, rs1_recv, rs2_send, rs2_recv, ag_send, ag_recv, fw_send, fw_recv, s_send, s_recv,
):
    d = lax.axis_index("dp")
    t = lax.axis_index("tile")
    n_chip = n_dp // 2
    core = lax.rem(d, 2)
    chip = lax.div(d, 2)
    left = (d, lax.rem(t + n_tile - 1, n_tile))
    right = (d, lax.rem(t + 1, n_tile))
    above = (d, lax.rem(t + n_tile - side, n_tile))
    below = (d, lax.rem(t + side, n_tile))
    sibling = (d + 1 - 2 * core, t)

    def at_chip(k):
        return (2 * k + core, t)

    n_x = n_chip // 2
    x_at = lax.div(chip, 2)
    y_at = lax.rem(chip, 2)
    along_x = sorted(range(n_x), key=lambda o: -min(o, n_x - o))
    steps = [(dx, 1) for dx in along_x] + [(dx, 0) for dx in along_x if dx]

    def chip_to(step):
        return 2 * lax.rem(x_at + step[0], n_x) + lax.rem(y_at + step[1], 2)

    def chip_from(step):
        return 2 * lax.rem(x_at + n_x - step[0], n_x) + lax.rem(y_at + step[1], 2)

    flips = []
    bit = 1
    while bit < n_chip:
        flips.append(at_chip(chip + bit - 2 * bit * lax.rem(lax.div(chip, bit), 2)))
        bit *= 2

    barrier = pltpu.get_barrier_semaphore()
    ahead = (d, lax.rem(t + 2, n_tile))
    behind = (d, lax.rem(t + n_tile - 2, n_tile))
    odd = lax.rem(t, 2)
    greeted = [right, below, left, ahead, sibling, *flips]
    for device in greeted:
        pl.semaphore_signal(barrier, inc=1, device_id=device, device_id_type=MESH)
    own_in = pltpu.make_async_copy(frames_ref, xext.at[:, pl.ds(0, PX), pl.ds(0, PX)], in_sem.at[0])
    own_in.start()
    weights_in = pltpu.make_async_copy(w_ref, w_in, in_sem.at[1])
    weights_in.start()
    pl.semaphore_wait(barrier, len(greeted))

    sent = []

    def remote(src, dst, send, recv, device):
        return pltpu.make_async_remote_copy(
            src_ref=src, dst_ref=dst, send_sem=send, recv_sem=recv, device_id=device, device_id_type=MESH
        )

    def start(copy, parity=None):
        if parity is None:
            copy.start()
        else:
            pl.when(odd == parity)(copy.start)
        sent.append((copy, parity))

    def start_left(direct, detour):
        start(direct, 1)
        start(detour, 0)

    def pass_on(arriving, onward):
        @pl.when(odd == 1)
        def _():
            arriving.wait_recv()
            onward.start()

        sent.append((onward, 1))

    def quarter(ext, low, far, q):
        return ext.at[:, pl.ds(PX * low + 4 * q, 4), pl.ds(PX * far, PX)]

    def halo(own, ext, hold, send, recv):
        to_left = [remote(own(q), quarter(ext, 0, 1, q), send.at[q], recv.at[q], left) for q in range(4)]
        to_above = [remote(own(q), quarter(ext, 1, 0, q), send.at[4 + q], recv.at[4 + q], above) for q in range(4)]
        relay = [
            remote(quarter(ext, 1, 0, q), quarter(ext, 1, 1, q), send.at[8 + q], recv.at[8 + q], left)
            for q in range(4)
        ]
        detour = [remote(own(q), hold.at[q], send.at[12 + q], recv.at[12 + q], right) for q in range(4)]
        onward = [remote(hold.at[q], quarter(ext, 0, 1, q), send.at[16 + q], recv.at[q], behind) for q in range(4)]
        return to_left, to_above, relay, detour, onward

    x_left, x_above, x_relay, x_detour, x_onward = halo(
        lambda q: frames_ref.at[:, pl.ds(4 * q, 4)], xext, x_hold, x_send, x_recv
    )
    for q in range(4):
        start(x_above[q])
    for q in range(4):
        start_left(x_left[q], x_detour[q])
    for device in flips:
        pl.semaphore_signal(tok.at[0], inc=1, device_id=device, device_id_type=MESH)

    lane = lax.broadcasted_iota(jnp.int32, (1, BAND), 1)
    chan = jnp.where(lane >= BLOCK, 1, 0) + jnp.where(lane >= 2 * BLOCK, 1, 0)
    spot = lane - BLOCK * chan
    prow = spot >> 5
    pcol = spot & 31
    source = jnp.where((pcol < FIELD) & (prow < FIELD), FIELD * FIELD * chan + FIELD * prow + pcol, -1)

    @pl.loop(0, WIDE // 32)
    def _(b):
        number = lax.broadcasted_iota(jnp.int32, (32, BAND), 0) + b * 32
        place[pl.ds(b * 32, 32), :] = jnp.where(number == source, 1.0, 0.0).astype(BF16)

    wpad[:, pl.ds(896, 128)] = jnp.zeros((128, 128), BF16)
    position = lax.broadcasted_iota(jnp.int32, (128, POS), 0) >> 3
    which = lax.broadcasted_iota(jnp.int32, (128, POS), 1)
    spans = ((0, 384), (256, 768), (640, 1024))
    weights_in.wait()

    def prepare(g):
        rows = pl.ds(g * 128, 128)
        wpad[:, pl.ds(0, INPUTS)] = w_in[pl.ds(g * 16, 16)].astype(F32).reshape(128, INPUTS).astype(BF16)
        for c in range(3):
            maps = conn_ref[c].astype(F32)
            tall = jnp.concatenate([maps] * 16, axis=0)
            picked = jnp.where(which == position + g * 16, tall, 0.0)
            opened[c, rows] = jnp.broadcast_to(jnp.sum(picked, axis=1, keepdims=True), (128, 128))
            lanes = pl.ds(c * BLOCK, BLOCK)
            lo, hi = spans[c]
            spread = dot(wpad[:, lo:hi], place[lo:hi, lanes]) * opened[c, rows][:, 0:1]
            rolled = []
            for p in range(16):
                shift = 64 * (p // 8) + 2 * (p % 8)
                part = spread[p * 8 : p * 8 + 8]
                rolled.append(pltpu.roll(part, shift, 1) if shift else part)
            whole = jnp.concatenate(rolled, axis=0)
            band[rows, lanes] = whole.astype(BF16)
            band_t[g, lanes, :] = whole.T.astype(BF16)

    prepare(0)
    for g in range(4):
        pass_on(x_detour[g], x_onward[g])
        x_above[g].wait_recv()
        start(x_relay[g])
        if g < 3:
            prepare(g + 1)
    pl.semaphore_wait(tok.at[0], len(flips))
    for device in flips:
        pl.semaphore_signal(tok.at[1], inc=1, device_id=device, device_id_type=MESH)
    dec[...] = jnp.zeros(dec.shape, F32)
    squares[3:] = jnp.zeros((5, 8, 128), F32)
    own_in.wait()

    def strip(ext, g):
        return ext[:, pl.ds(4 * g, 20)].reshape(BAND, 128)

    fold_right = [
        remote(right_src.at[q], right_in.at[q], f_send.at[q], f_recv.at[q], right) for q in range(4)
    ]
    fold_corner = [
        remote(corner_src.at[q], corner_in.at[q], f_send.at[4 + q], f_recv.at[4 + q], right) for q in range(4)
    ]
    fold_below = [
        remote(below_src.at[q], below_in.at[q], f_send.at[8 + q], f_recv.at[8 + q], below) for q in range(4)
    ]
    for g in range(4):
        x_left[g].wait_recv()
    for g in range(4):
        x_relay[g].wait_recv()
        rows = pl.ds(g * 128, 128)
        value = dot(band[rows, :], strip(xext, g))
        rounded = value.astype(BF16)
        coded[rows] = value
        coded_b[rows] = rounded
        dec[:, pl.ds(4 * g, 20)] += dot(band_t[g], rounded).reshape(3, 20, 32, 128)
        if g < 3:
            right_src[g] = dec[:, pl.ds(4 * g, 4), pl.ds(PX, PX)].astype(BF16)
            start(fold_right[g])
    for q in range(4):
        corner_src[q] = dec[:, pl.ds(PX + 4 * q, 4), pl.ds(PX, PX)].astype(BF16)
        start(fold_corner[q])
    right_src[3] = dec[:, pl.ds(12, 4), pl.ds(PX, PX)].astype(BF16)
    start(fold_right[3])
    for q in range(4):
        fold_corner[q].wait_recv()
        summed = dec[:, pl.ds(PX + 4 * q, 4), pl.ds(0, PX)] + corner_in[q].astype(F32)
        below_src[q] = summed.astype(BF16)
        start(fold_below[q])

    value = coded[...]
    penalty = jnp.sqrt(smooth_eps + value * value)
    squares[2] = jnp.sum(penalty.reshape(ROWS // 8, 8, 128), axis=0)
    pl.semaphore_wait(tok.at[1], len(flips))

    e_left, e_above, e_relay, e_detour, e_onward = halo(
        lambda q: quarter(eext, 0, 0, q), eext, e_hold, e_send, e_recv
    )
    error_sq = jnp.zeros((16, 128), F32)
    for q in range(4):
        fold_right[q].wait_recv()
        fold_below[q].wait_recv()
        own = (slice(None), pl.ds(4 * q, 4), pl.ds(0, PX))
        rebuilt = dec[own] + right_in[q].astype(F32) + below_in[q].astype(F32)
        error = rebuilt - xext[own].astype(F32)
        error_sq = error_sq + jnp.sum(error * error, axis=(0, 1))
        eext[own] = error.astype(BF16)
        start(e_above[q])
        start_left(e_left[q], e_detour[q])
        if q > 0:
            pass_on(e_detour[q - 1], e_onward[q - 1])
        if q > 1:
            e_above[q - 2].wait_recv()
            start(e_relay[q - 2])
    pass_on(e_detour[3], e_onward[3])
    for q in (2, 3):
        e_above[q].wait_recv()
        start(e_relay[q])
    squares[1] = error_sq[:8] + error_sq[8:]
    for q in range(4):
        e_left[q].wait_recv()

    def finish(g):
        rows = pl.ds(g * 128, 128)
        errors = strip(eext, g)
        value = coded[rows]
        enc = dot(band[rows, :], errors)
        coef = (2.0 * enc + value * lax.rsqrt(smooth_eps + value * value)).astype(BF16)
        both = jnp.concatenate([coded_b[rows] * 2, coef], axis=1)
        parts = []
        for c in range(3):
            lanes = slice(c * BLOCK, (c + 1) * BLOCK)
            patch = jnp.concatenate(
                [ext[c, pl.ds(4 * g, 20)].reshape(BLOCK, 128) for ext in (eext, xext)], axis=1
            )
            whole = dot_nt(both, patch) * opened[c, rows][:, 0:1]
            rolled = []
            for p in range(16):
                shift = 64 * (p // 8) + 2 * (p % 8)
                part = whole[p * 8 : p * 8 + 8]
                rolled.append(pltpu.roll(part, BLOCK - shift, 1) if shift else part)
            gband[...] = jnp.concatenate(rolled, axis=0).astype(BF16)
            lo, hi = spans[c]
            parts.append(dot_nt(gband[...], place[lo:hi, lanes]))
        first, middle, last = parts
        gsend[g, :, 0:256] = first[:, :256].astype(BF16)
        gsend[g, :, 256:384] = (first[:, 256:] + middle[:, :128]).astype(BF16)
        gsend[g, :, 384:640] = middle[:, 128:384].astype(BF16)
        gsend[g, :, 640:768] = (middle[:, 384:] + last[:, :128]).astype(BF16)
        gsend[g, :, 768:1024] = last[:, 128:].astype(BF16)

    def half_of(k):
        return pl.ds(pl.multiple_of(k * 64, 64), 64)

    def lanes_of(k):
        return pl.ds(pl.multiple_of(k * 128, 128), 128)

    swap = [
        remote(gsend.at[g, half_of(1 - core)], rs_in.at[g], rs1_send.at[g], rs1_recv.at[g], sibling)
        for g in range(4)
    ]
    scatter = []

    def combine(batch_no):
        for g in (2 * batch_no, 2 * batch_no + 1):
            swap[g].wait_recv()
            rs_half[g] = (gsend[g, half_of(core)].astype(F32) + rs_in[g].astype(F32)).astype(BF16)
        for o, step in enumerate(steps, 1):
            to = chip_to(step)
            n = batch_no * (n_chip - 1) + o - 1
            copy = remote(
                rs_half.at[pl.ds(2 * batch_no, 2), :, lanes_of(to)],
                rs_parts.at[o - 1, pl.ds(2 * batch_no, 2)],
                rs2_send.at[n], rs2_recv.at[n], at_chip(to),
            )
            start(copy)
            scatter.append(copy)

    for g in range(4):
        e_relay[g].wait_recv()
        finish(g)
        start(swap[g])
        if g == 2:
            combine(0)
    combine(1)

    def place_of(batch_no, k):
        return gathered.at[pl.ds(2 * batch_no, 2), core, :, lanes_of(k)]

    spread_out = [[], []]
    forward = []

    def pass_to_sibling(batch_no, k, o):
        n = batch_no * n_chip + o
        block = place_of(batch_no, k)
        copy = remote(block, block, fw_send.at[n], fw_recv.at[n], sibling)
        start(copy)
        forward.append(copy)

    def gather(batch_no):
        block = place_of(batch_no, chip)
        for o, step in enumerate(steps, 1):
            n = batch_no * (n_chip - 1) + o - 1
            to = chip_to(step)
            copy = remote(block, block, ag_send.at[n], ag_recv.at[n], at_chip(to))
            start(copy)
            spread_out[batch_no].append(copy)
        pass_to_sibling(batch_no, chip, 0)

    def hand_on(batch_no):
        for o in reversed(range(1, n_chip)):
            spread_out[batch_no][o - 1].wait_recv()
            pass_to_sibling(batch_no, chip_from(steps[o - 1]), o)

    def add_up(batch_no):
        pair = pl.ds(2 * batch_no, 2)
        share = rs_half[pair, :, lanes_of(chip)].astype(F32)
        for o in range(1, n_chip):
            scatter[batch_no * (n_chip - 1) + o - 1].wait_recv()
            share = share + rs_parts[o - 1, pair].astype(F32)
        gathered[pair, core, :, lanes_of(chip)] = share.astype(BF16)
        return jnp.sum((share * share).reshape(16, 8, 128), axis=0)

    square = add_up(0)
    gather(0)
    squares[0] = square + add_up(1)

    total = jnp.sum(squares[...], axis=1)
    scal[0] = total

    def exchange(stage, targets, first):
        copies = []
        for n, device in enumerate(targets):
            copy = remote(
                scal.at[stage], scal_in.at[first + n], s_send.at[first + n], s_recv.at[first + n], device
            )
            start(copy)
            copies.append(copy)
        return copies

    def collect(total, copies, first):
        for n, copy in enumerate(copies):
            copy.wait_recv()
            total = total + scal_in[first + n]
        return total

    rounds = [
        [(2 * chip_to(step) + lax.rem(core + o, 2), t) for step in steps for o in (1, 0)] + [sibling],
        [(d, lax.rem(t + o, n_tile)) for o in sorted(range(1, n_tile), key=lambda o: -min(o, n_tile - o))],
    ]
    copies = exchange(0, rounds[0], 0)
    gather(1)
    first = 0
    for stage in range(1, len(rounds)):
        total = collect(total, copies, first)
        first += len(copies)
        scal[stage] = total
        copies = exchange(stage, rounds[stage], first)
    hand_on(0)
    hand_on(1)
    total = collect(total, copies, first)
    sums = jnp.sum(total, axis=1, keepdims=True)
    factor = lax.rsqrt(sums[0:1] / (n_tile * ROWS * INPUTS) + guard_eps)
    loss_ref[...] = jnp.broadcast_to((sums[1:2] + sums[2:3]) / batch, loss_ref.shape)
    for copy in forward:
        copy.wait_recv()
    out_ref[...] = (-(gathered[...].reshape(ROWS, WIDE).astype(F32) * factor)).astype(BF16)
    for copy, parity in sent:
        if parity is None:
            copy.wait_send()
        else:
            pl.when(odd == parity)(copy.wait_send)


def local(n_dp, n_tile, side, frames, weights, connect):
    n_chip = n_dp // 2
    batch = frames.shape[-1] * n_dp
    dma = pltpu.SemaphoreType.DMA
    vmem = pl.BlockSpec(memory_space=pltpu.VMEM)
    hbm = pl.BlockSpec(memory_space=pltpu.HBM)
    n_small = n_dp + n_tile - 2
    scratch = [
        pltpu.VMEM((POS, MAPS, INPUTS), BF16),
        pltpu.VMEM((3, ROWS, 128), F32),
        pltpu.VMEM((WIDE, BAND), BF16),
        pltpu.VMEM((128, WIDE), BF16),
        pltpu.VMEM((ROWS, BAND), BF16),
        pltpu.VMEM((GROUPS, BAND, 128), BF16),
        pltpu.VMEM((3, 32, 32, 128), BF16),
        pltpu.VMEM((3, 32, 32, 128), BF16),
        pltpu.VMEM((ROWS, 128), F32),
        pltpu.VMEM((ROWS, 128), BF16),
        pltpu.VMEM((3, 32, 32, 128), F32),
        *[pltpu.VMEM((4, 3, 4, PX, 128), BF16) for _ in range(6)],
        *[pltpu.VMEM((4, 3, 4, PX, 128), BF16) for _ in range(2)],
        pltpu.VMEM((128, BLOCK), BF16),
        pltpu.VMEM((GROUPS, 128, WIDE), BF16),
        pltpu.VMEM((GROUPS, 64, WIDE), BF16),
        pltpu.VMEM((GROUPS, 64, WIDE), BF16),
        pltpu.VMEM((n_chip - 1, GROUPS, 64, 128), BF16),
        pltpu.VMEM((GROUPS, 2, 64, WIDE), BF16),
        pltpu.VMEM((8, 8, 128), F32),
        pltpu.VMEM((4, 8, 128), F32),
        pltpu.VMEM((n_small, 8, 128), F32),
        dma((2,)),
        pltpu.SemaphoreType.REGULAR((2,)),
        *[dma((20,)) for _ in range(6)],
        dma((4,)), dma((4,)),
        dma((2 * (n_chip - 1),)), dma((2 * (n_chip - 1),)),
        dma((2 * (n_chip - 1),)), dma((2 * (n_chip - 1),)),
        dma((2 * n_chip,)), dma((2 * n_chip,)),
        dma((n_small,)), dma((n_small,)),
    ]
    update, loss = pl.pallas_call(
        functools.partial(kernel, n_dp, n_tile, batch, side),
        out_shape=(
            jax.ShapeDtypeStruct((ROWS, WIDE), BF16),
            jax.ShapeDtypeStruct((8, 128), F32),
        ),
        in_specs=[hbm, hbm, vmem],
        out_specs=(vmem, vmem),
        scratch_shapes=scratch,
        compiler_params=pltpu.CompilerParams(
            collective_id=0, has_side_effects=True, vmem_limit_bytes=54000 * 1024
        ),
    )(frames[0], weights[0], jnp.transpose(connect[0], (2, 1, 0)))
    return update[:, :INPUTS].reshape(1, POS, MAPS, INPUTS), loss[0, 0]


def solution(mesh):
    n_dp, n_tile = mesh.shape["dp"], mesh.shape["tile"]
    side = int(round(n_tile ** 0.5))
    in_specs = (P("tile", None, None, None, "dp"), P("tile", None, None, None), P("tile", None, None, None))
    out_specs = (P("tile", None, None, None), P())
    return jax.shard_map(
        functools.partial(local, n_dp, n_tile, side), mesh=mesh, in_specs=in_specs, out_specs=out_specs, check_vma=False
    )
```

```python
import functools

import jax
import jax.numpy as jnp
from jax import lax
from jax.experimental import pallas as pl
from jax.experimental.pallas import tpu as pltpu
from jax.sharding import PartitionSpec as P

FIELD = 18
MAPS = 8
INPUTS = 972
POS = 64
PX = 16
BLOCK = 640
BAND = 3 * BLOCK
ROWS = POS * MAPS
WIDE = 1024
GROUPS = 4
MESH = pl.DeviceIdType.MESH
F32 = jnp.float32
BF16 = jnp.bfloat16

smooth_eps = 0.01
guard_eps = 1e-06


def dot(a, b):
    return lax.dot_general(a, b, (((1,), (0,)), ((), ())), preferred_element_type=F32)


def dot_nt(a, b):
    return lax.dot_general(a, b, (((1,), (1,)), ((), ())), preferred_element_type=F32)


def kernel(
    n_dp, n_tile, batch, side,
    frames_ref, w_ref, conn_ref,
    out_ref, loss_ref,
    w_in, opened, place, wpad, band, band_t, xext, eext, coded, coded_b, dec,
    right_src, right_in, corner_src, corner_in, below_src, below_in,
    x_hold, e_hold, gband, gsend, rs_in, rs_half, rs_parts, gathered,
    squares, scal, scal_in,
    in_sem, tok,
    x_send, x_recv, f_send, f_recv, e_send, e_recv,
    rs1_send, rs1_recv, rs2_send, rs2_recv, ag_send, ag_recv, fw_send, fw_recv, s_send, s_recv,
):
    d = lax.axis_index("dp")
    t = lax.axis_index("tile")
    n_chip = n_dp // 2
    core = lax.rem(d, 2)
    chip = lax.div(d, 2)
    left = (d, lax.rem(t + n_tile - 1, n_tile))
    right = (d, lax.rem(t + 1, n_tile))
    above = (d, lax.rem(t + n_tile - side, n_tile))
    below = (d, lax.rem(t + side, n_tile))
    sibling = (d + 1 - 2 * core, t)

    def at_chip(k):
        return (2 * k + core, t)

    n_x = n_chip // 2
    x_at = lax.div(chip, 2)
    y_at = lax.rem(chip, 2)
    along_x = sorted(range(n_x), key=lambda o: -min(o, n_x - o))
    steps = [(dx, 1) for dx in along_x] + [(dx, 0) for dx in along_x if dx]

    def chip_to(step):
        return 2 * lax.rem(x_at + step[0], n_x) + lax.rem(y_at + step[1], 2)

    def chip_from(step):
        return 2 * lax.rem(x_at + n_x - step[0], n_x) + lax.rem(y_at + step[1], 2)

    flips = []
    bit = 1
    while bit < n_chip:
        flips.append(at_chip(chip + bit - 2 * bit * lax.rem(lax.div(chip, bit), 2)))
        bit *= 2

    barrier = pltpu.get_barrier_semaphore()
    ahead = (d, lax.rem(t + 2, n_tile))
    behind = (d, lax.rem(t + n_tile - 2, n_tile))
    odd = lax.rem(t, 2)
    greeted = [right, below, left, ahead, sibling, *flips]
    for device in greeted:
        pl.semaphore_signal(barrier, inc=1, device_id=device, device_id_type=MESH)
    own_in = pltpu.make_async_copy(frames_ref, xext.at[:, pl.ds(0, PX), pl.ds(0, PX)], in_sem.at[0])
    own_in.start()
    weights_in = pltpu.make_async_copy(w_ref, w_in, in_sem.at[1])
    weights_in.start()
    pl.semaphore_wait(barrier, len(greeted))

    sent = []

    def remote(src, dst, send, recv, device):
        return pltpu.make_async_remote_copy(
            src_ref=src, dst_ref=dst, send_sem=send, recv_sem=recv, device_id=device, device_id_type=MESH
        )

    def start(copy, parity=None):
        if parity is None:
            copy.start()
        else:
            pl.when(odd == parity)(copy.start)
        sent.append((copy, parity))

    def start_left(direct, detour):
        start(direct, 1)
        start(detour, 0)

    def pass_on(arriving, onward):
        @pl.when(odd == 1)
        def _():
            arriving.wait_recv()
            onward.start()

        sent.append((onward, 1))

    def quarter(ext, low, far, q):
        return ext.at[:, pl.ds(PX * low + 4 * q, 4), pl.ds(PX * far, PX)]

    def halo(own, ext, hold, send, recv):
        to_left = [remote(own(q), quarter(ext, 0, 1, q), send.at[q], recv.at[q], left) for q in range(4)]
        to_above = [remote(own(q), quarter(ext, 1, 0, q), send.at[4 + q], recv.at[4 + q], above) for q in range(4)]
        relay = [
            remote(quarter(ext, 1, 0, q), quarter(ext, 1, 1, q), send.at[8 + q], recv.at[8 + q], left)
            for q in range(4)
        ]
        detour = [remote(own(q), hold.at[q], send.at[12 + q], recv.at[12 + q], right) for q in range(4)]
        onward = [remote(hold.at[q], quarter(ext, 0, 1, q), send.at[16 + q], recv.at[q], behind) for q in range(4)]
        return to_left, to_above, relay, detour, onward

    x_left, x_above, x_relay, x_detour, x_onward = halo(
        lambda q: frames_ref.at[:, pl.ds(4 * q, 4)], xext, x_hold, x_send, x_recv
    )
    for q in range(4):
        start(x_above[q])
    for q in range(4):
        start_left(x_left[q], x_detour[q])
    for device in flips:
        pl.semaphore_signal(tok.at[0], inc=1, device_id=device, device_id_type=MESH)

    lane = lax.broadcasted_iota(jnp.int32, (1, BAND), 1)
    chan = jnp.where(lane >= BLOCK, 1, 0) + jnp.where(lane >= 2 * BLOCK, 1, 0)
    spot = lane - BLOCK * chan
    prow = spot >> 5
    pcol = spot & 31
    source = jnp.where((pcol < FIELD) & (prow < FIELD), FIELD * FIELD * chan + FIELD * prow + pcol, -1)

    @pl.loop(0, WIDE // 32)
    def _(b):
        number = lax.broadcasted_iota(jnp.int32, (32, BAND), 0) + b * 32
        place[pl.ds(b * 32, 32), :] = jnp.where(number == source, 1.0, 0.0).astype(BF16)

    wpad[:, pl.ds(896, 128)] = jnp.zeros((128, 128), BF16)
    position = lax.broadcasted_iota(jnp.int32, (128, POS), 0) >> 3
    which = lax.broadcasted_iota(jnp.int32, (128, POS), 1)
    spans = ((0, 384), (256, 768), (640, 1024))
    weights_in.wait()

    def prepare(g):
        rows = pl.ds(g * 128, 128)
        wpad[:, pl.ds(0, INPUTS)] = w_in[pl.ds(g * 16, 16)].astype(F32).reshape(128, INPUTS).astype(BF16)
        for c in range(3):
            maps = conn_ref[c].astype(F32)
            tall = jnp.concatenate([maps] * 16, axis=0)
            picked = jnp.where(which == position + g * 16, tall, 0.0)
            opened[c, rows] = jnp.broadcast_to(jnp.sum(picked, axis=1, keepdims=True), (128, 128))
            lanes = pl.ds(c * BLOCK, BLOCK)
            lo, hi = spans[c]
            spread = dot(wpad[:, lo:hi], place[lo:hi, lanes]) * opened[c, rows][:, 0:1]
            rolled = []
            for p in range(16):
                shift = 64 * (p // 8) + 2 * (p % 8)
                part = spread[p * 8 : p * 8 + 8]
                rolled.append(pltpu.roll(part, shift, 1) if shift else part)
            whole = jnp.concatenate(rolled, axis=0)
            band[rows, lanes] = whole.astype(BF16)
            band_t[g, lanes, :] = whole.T.astype(BF16)

    prepare(0)
    for g in range(4):
        x_above[g].wait_recv()
        start(x_relay[g])
        if g < 3:
            prepare(g + 1)
        pass_on(x_detour[g], x_onward[g])
    pl.semaphore_wait(tok.at[0], len(flips))
    for device in flips:
        pl.semaphore_signal(tok.at[1], inc=1, device_id=device, device_id_type=MESH)
    dec[...] = jnp.zeros(dec.shape, F32)
    squares[3:] = jnp.zeros((5, 8, 128), F32)
    own_in.wait()

    def strip(ext, g):
        return ext[:, pl.ds(4 * g, 20)].reshape(BAND, 128)

    fold_right = [
        remote(right_src.at[q], right_in.at[q], f_send.at[q], f_recv.at[q], right) for q in range(4)
    ]
    fold_corner = [
        remote(corner_src.at[q], corner_in.at[q], f_send.at[4 + q], f_recv.at[4 + q], right) for q in range(4)
    ]
    fold_below = [
        remote(below_src.at[q], below_in.at[q], f_send.at[8 + q], f_recv.at[8 + q], below) for q in range(4)
    ]
    for g in range(4):
        x_left[g].wait_recv()
    for g in range(4):
        x_relay[g].wait_recv()
        rows = pl.ds(g * 128, 128)
        value = dot(band[rows, :], strip(xext, g))
        rounded = value.astype(BF16)
        coded[rows] = value
        coded_b[rows] = rounded
        dec[:, pl.ds(4 * g, 20)] += dot(band_t[g], rounded).reshape(3, 20, 32, 128)
        if g < 3:
            right_src[g] = dec[:, pl.ds(4 * g, 4), pl.ds(PX, PX)].astype(BF16)
            start(fold_right[g])
    for q in range(4):
        corner_src[q] = dec[:, pl.ds(PX + 4 * q, 4), pl.ds(PX, PX)].astype(BF16)
        start(fold_corner[q])
    right_src[3] = dec[:, pl.ds(12, 4), pl.ds(PX, PX)].astype(BF16)
    start(fold_right[3])
    for q in range(4):
        fold_corner[q].wait_recv()
        summed = dec[:, pl.ds(PX + 4 * q, 4), pl.ds(0, PX)] + corner_in[q].astype(F32)
        below_src[q] = summed.astype(BF16)
        start(fold_below[q])

    value = coded[...]
    penalty = jnp.sqrt(smooth_eps + value * value)
    squares[2] = jnp.sum(penalty.reshape(ROWS // 8, 8, 128), axis=0)
    pl.semaphore_wait(tok.at[1], len(flips))

    e_left, e_above, e_relay, e_detour, e_onward = halo(
        lambda q: quarter(eext, 0, 0, q), eext, e_hold, e_send, e_recv
    )
    error_sq = jnp.zeros((16, 128), F32)
    for q in range(4):
        fold_right[q].wait_recv()
        fold_below[q].wait_recv()
        own = (slice(None), pl.ds(4 * q, 4), pl.ds(0, PX))
        rebuilt = dec[own] + right_in[q].astype(F32) + below_in[q].astype(F32)
        error = rebuilt - xext[own].astype(F32)
        error_sq = error_sq + jnp.sum(error * error, axis=(0, 1))
        eext[own] = error.astype(BF16)
        start(e_above[q])
        start_left(e_left[q], e_detour[q])
        if q > 0:
            pass_on(e_detour[q - 1], e_onward[q - 1])
        if q > 1:
            e_above[q - 2].wait_recv()
            start(e_relay[q - 2])
    pass_on(e_detour[3], e_onward[3])
    for q in (2, 3):
        e_above[q].wait_recv()
        start(e_relay[q])
    squares[1] = error_sq[:8] + error_sq[8:]
    for q in range(4):
        e_left[q].wait_recv()

    def finish(g):
        rows = pl.ds(g * 128, 128)
        errors = strip(eext, g)
        value = coded[rows]
        enc = dot(band[rows, :], errors)
        coef = (2.0 * enc + value * lax.rsqrt(smooth_eps + value * value)).astype(BF16)
        both = jnp.concatenate([coded_b[rows] * 2, coef], axis=1)
        parts = []
        for c in range(3):
            lanes = slice(c * BLOCK, (c + 1) * BLOCK)
            patch = jnp.concatenate(
                [ext[c, pl.ds(4 * g, 20)].reshape(BLOCK, 128) for ext in (eext, xext)], axis=1
            )
            whole = dot_nt(both, patch) * opened[c, rows][:, 0:1]
            rolled = []
            for p in range(16):
                shift = 64 * (p // 8) + 2 * (p % 8)
                part = whole[p * 8 : p * 8 + 8]
                rolled.append(pltpu.roll(part, BLOCK - shift, 1) if shift else part)
            gband[...] = jnp.concatenate(rolled, axis=0).astype(BF16)
            lo, hi = spans[c]
            parts.append(dot_nt(gband[...], place[lo:hi, lanes]))
        first, middle, last = parts
        gsend[g, :, 0:256] = first[:, :256].astype(BF16)
        gsend[g, :, 256:384] = (first[:, 256:] + middle[:, :128]).astype(BF16)
        gsend[g, :, 384:640] = middle[:, 128:384].astype(BF16)
        gsend[g, :, 640:768] = (middle[:, 384:] + last[:, :128]).astype(BF16)
        gsend[g, :, 768:1024] = last[:, 128:].astype(BF16)

    def half_of(k):
        return pl.ds(pl.multiple_of(k * 64, 64), 64)

    def lanes_of(k):
        return pl.ds(pl.multiple_of(k * 128, 128), 128)

    swap = [
        remote(gsend.at[g, half_of(1 - core)], rs_in.at[g], rs1_send.at[g], rs1_recv.at[g], sibling)
        for g in range(4)
    ]
    scatter = []

    def combine(batch_no):
        for g in (2 * batch_no, 2 * batch_no + 1):
            swap[g].wait_recv()
            rs_half[g] = (gsend[g, half_of(core)].astype(F32) + rs_in[g].astype(F32)).astype(BF16)
        for o, step in enumerate(steps, 1):
            to = chip_to(step)
            n = batch_no * (n_chip - 1) + o - 1
            copy = remote(
                rs_half.at[pl.ds(2 * batch_no, 2), :, lanes_of(to)],
                rs_parts.at[o - 1, pl.ds(2 * batch_no, 2)],
                rs2_send.at[n], rs2_recv.at[n], at_chip(to),
            )
            start(copy)
            scatter.append(copy)

    for g in range(4):
        e_relay[g].wait_recv()
        finish(g)
        start(swap[g])
        if g == 2:
            combine(0)
    combine(1)

    def place_of(batch_no, k):
        return gathered.at[pl.ds(2 * batch_no, 2), core, :, lanes_of(k)]

    spread_out = [[], []]
    forward = []

    def pass_to_sibling(batch_no, k, o):
        n = batch_no * n_chip + o
        block = place_of(batch_no, k)
        copy = remote(block, block, fw_send.at[n], fw_recv.at[n], sibling)
        start(copy)
        forward.append(copy)

    def gather(batch_no):
        block = place_of(batch_no, chip)
        for o, step in enumerate(steps, 1):
            n = batch_no * (n_chip - 1) + o - 1
            to = chip_to(step)
            copy = remote(block, block, ag_send.at[n], ag_recv.at[n], at_chip(to))
            start(copy)
            spread_out[batch_no].append(copy)
        pass_to_sibling(batch_no, chip, 0)

    def hand_on(batch_no):
        for o in reversed(range(1, n_chip)):
            spread_out[batch_no][o - 1].wait_recv()
            pass_to_sibling(batch_no, chip_from(steps[o - 1]), o)

    def add_up(batch_no):
        pair = pl.ds(2 * batch_no, 2)
        share = rs_half[pair, :, lanes_of(chip)].astype(F32)
        for o in range(1, n_chip):
            scatter[batch_no * (n_chip - 1) + o - 1].wait_recv()
            share = share + rs_parts[o - 1, pair].astype(F32)
        gathered[pair, core, :, lanes_of(chip)] = share.astype(BF16)
        return jnp.sum((share * share).reshape(16, 8, 128), axis=0)

    square = add_up(0)
    gather(0)
    squares[0] = square + add_up(1)

    total = jnp.sum(squares[...], axis=1)
    scal[0] = total

    def exchange(stage, targets, first):
        copies = []
        for n, device in enumerate(targets):
            copy = remote(
                scal.at[stage], scal_in.at[first + n], s_send.at[first + n], s_recv.at[first + n], device
            )
            start(copy)
            copies.append(copy)
        return copies

    def collect(total, copies, first):
        for n, copy in enumerate(copies):
            copy.wait_recv()
            total = total + scal_in[first + n]
        return total

    rounds = [
        [(2 * chip_to(step) + lax.rem(core + o, 2), t) for step in steps for o in (1, 0)] + [sibling],
        [(d, lax.rem(t + o, n_tile)) for o in sorted(range(1, n_tile), key=lambda o: -min(o, n_tile - o))],
    ]
    copies = exchange(0, rounds[0], 0)
    gather(1)
    first = 0
    for stage in range(1, len(rounds)):
        total = collect(total, copies, first)
        first += len(copies)
        scal[stage] = total
        copies = exchange(stage, rounds[stage], first)
    hand_on(0)
    hand_on(1)
    total = collect(total, copies, first)
    sums = jnp.sum(total, axis=1, keepdims=True)
    factor = lax.rsqrt(sums[0:1] / (n_tile * ROWS * INPUTS) + guard_eps)
    loss_ref[...] = jnp.broadcast_to((sums[1:2] + sums[2:3]) / batch, loss_ref.shape)
    for copy in forward:
        copy.wait_recv()
    out_ref[...] = (-(gathered[...].reshape(ROWS, WIDE).astype(F32) * factor)).astype(BF16)
    for copy, parity in sent:
        if parity is None:
            copy.wait_send()
        else:
            pl.when(odd == parity)(copy.wait_send)


def local(n_dp, n_tile, side, frames, weights, connect):
    n_chip = n_dp // 2
    batch = frames.shape[-1] * n_dp
    dma = pltpu.SemaphoreType.DMA
    vmem = pl.BlockSpec(memory_space=pltpu.VMEM)
    hbm = pl.BlockSpec(memory_space=pltpu.HBM)
    n_small = n_dp + n_tile - 2
    scratch = [
        pltpu.VMEM((POS, MAPS, INPUTS), BF16),
        pltpu.VMEM((3, ROWS, 128), F32),
        pltpu.VMEM((WIDE, BAND), BF16),
        pltpu.VMEM((128, WIDE), BF16),
        pltpu.VMEM((ROWS, BAND), BF16),
        pltpu.VMEM((GROUPS, BAND, 128), BF16),
        pltpu.VMEM((3, 32, 32, 128), BF16),
        pltpu.VMEM((3, 32, 32, 128), BF16),
        pltpu.VMEM((ROWS, 128), F32),
        pltpu.VMEM((ROWS, 128), BF16),
        pltpu.VMEM((3, 32, 32, 128), F32),
        *[pltpu.VMEM((4, 3, 4, PX, 128), BF16) for _ in range(6)],
        *[pltpu.VMEM((4, 3, 4, PX, 128), BF16) for _ in range(2)],
        pltpu.VMEM((128, BLOCK), BF16),
        pltpu.VMEM((GROUPS, 128, WIDE), BF16),
        pltpu.VMEM((GROUPS, 64, WIDE), BF16),
        pltpu.VMEM((GROUPS, 64, WIDE), BF16),
        pltpu.VMEM((n_chip - 1, GROUPS, 64, 128), BF16),
        pltpu.VMEM((GROUPS, 2, 64, WIDE), BF16),
        pltpu.VMEM((8, 8, 128), F32),
        pltpu.VMEM((4, 8, 128), F32),
        pltpu.VMEM((n_small, 8, 128), F32),
        dma((2,)),
        pltpu.SemaphoreType.REGULAR((2,)),
        *[dma((20,)) for _ in range(6)],
        dma((4,)), dma((4,)),
        dma((2 * (n_chip - 1),)), dma((2 * (n_chip - 1),)),
        dma((2 * (n_chip - 1),)), dma((2 * (n_chip - 1),)),
        dma((2 * n_chip,)), dma((2 * n_chip,)),
        dma((n_small,)), dma((n_small,)),
    ]
    update, loss = pl.pallas_call(
        functools.partial(kernel, n_dp, n_tile, batch, side),
        out_shape=(
            jax.ShapeDtypeStruct((ROWS, WIDE), BF16),
            jax.ShapeDtypeStruct((8, 128), F32),
        ),
        in_specs=[hbm, hbm, vmem],
        out_specs=(vmem, vmem),
        scratch_shapes=scratch,
        compiler_params=pltpu.CompilerParams(
            collective_id=0, has_side_effects=True, vmem_limit_bytes=54000 * 1024
        ),
    )(frames[0], weights[0], jnp.transpose(connect[0], (2, 1, 0)))
    return update[:, :INPUTS].reshape(1, POS, MAPS, INPUTS), loss[0, 0]


def solution(mesh):
    n_dp, n_tile = mesh.shape["dp"], mesh.shape["tile"]
    side = int(round(n_tile ** 0.5))
    in_specs = (P("tile", None, None, None, "dp"), P("tile", None, None, None), P("tile", None, None, None))
    out_specs = (P("tile", None, None, None), P())
    return jax.shard_map(
        functools.partial(local, n_dp, n_tile, side), mesh=mesh, in_specs=in_specs, out_specs=out_specs, check_vma=False
    )
```
